256 devices in a mesh: ctx: 64 (over x, y, z_lo, core), tp: 4 (over z_hi).
Axes of the slice: x: 4, y: 4, z: 8 (z_hi: 4, z_lo: 2; z = z_hi * 2 + z_lo), core: 2. Of those that a mesh axis runs over, the one named last changes fastest.
Arguments:
- hidden: bfloat16 [1, 16384, 8192], P(None, 'ctx', 'tp'), may hold values from -6 to 6
- doc_lengths: int32 [1, 128], replicated, may hold values from 1 to 512, 16384 in all within a row
- gain_se: float32 [8192], P('tp'), may hold values from 0.5 to 1.5
- gain_mr: float32 [8192], P('tp'), may hold values from 0.5 to 1.5
- feat_se: float32 [3, 3, 8192], P(None, None, 'tp'), may hold values from -4 to 4
- feat_mr: float32 [3, 3, 8192], P(None, None, 'tp'), may hold values from -4 to 4
- filter_se: float32 [512, 7], P('tp'), may hold values from -3 to 3
- filter_mr: bfloat16 [512, 128], P('tp'), may hold values from -0.5 to 0.5
Outputs:
- output: bfloat16 [1, 16384, 8192], P(None, 'ctx', 'tp')
The draws below stay inside these ranges and needn't reach their ends.
Inputs may be any that keep to these rules, and one draw needn't show every extreme that they name: `doc_lengths`: each row lists document lengths that sum to 16384; the longest is exactly 512.
All inputs are finite; a program needn't handle non-finite values.
Results may differ from the reference program's by a relative error of at most 0.03.
Values may be sent and summed in bfloat16 or wider, within the bound.
No kernel may reach another device: no remote copies, remote signals or barrier semaphores. Data moves between devices by JAX's collectives and lax.ppermute only.
A program may use at most 128 MiB of HBM per device.

```python
import math
import jax
import jax.numpy as jnp
import numpy as np
from jax import lax

D = 8192
GROUPS = 512
FEAT_TAPS = 3
SHORT_TAPS = 7
MEDIUM_TAPS = 128
SEQS = 1
TOKENS = 16384
NDOC = 128
MAXDOC = 512


def block_levels(stream_key, dims, split, low, high):
    level = 1.0
    for axis_at, shards_of in split:
        heights = jax.random.uniform(jax.random.fold_in(jax.random.fold_in(stream_key, 6), axis_at), (shards_of,), jnp.float32, low / len(split), high / len(split))
        level = level * jnp.repeat(jnp.exp(heights), dims[axis_at] // shards_of).reshape((-1,) + (1,) * (len(dims) - 1 - axis_at))
    return level


def profile(number_of, total, bound, slope):
    weights = [(1 << 20) // math.isqrt(grade ** slope) + 1 for grade in range(2, number_of + 1)]
    spare, counts = total - bound - (number_of - 1), [1] * (number_of - 1)
    while spare > 0:
        candidates = [i for i in range(number_of - 1) if counts[i] < bound]
        pool, budget = sum([weights[i] for i in candidates]), spare
        for i in candidates:
            extra = min(bound - counts[i], max(1, budget * weights[i] // pool), spare)
            counts[i] = counts[i] + extra
            spare = spare - extra
    return np.array([bound] + counts)


def ragged_sizes(key, amount, total, most, lean):
    if amount == 2:
        one = jax.random.randint(key, (), max(1, total - most), min(most, total - 1) + 1)
        return jnp.stack([one, total - one])
    sizes = jnp.asarray(profile(amount, total, most, lean), jnp.int32)
    couples = (amount - 1) // 2
    giver, sink = sizes[1:1 + 2 * couples:2], sizes[2:2 + 2 * couples:2]
    room = jnp.minimum(giver - 1, most - sink)
    moved = jax.random.randint(jax.random.fold_in(key, 1), (couples,), 0, 1 << 20) % (room + 1)
    sizes = sizes.at[1:1 + 2 * couples:2].set(giver - moved).at[2:2 + 2 * couples:2].set(sink + moved)
    return sizes[jax.random.permutation(jax.random.fold_in(key, 2), amount)]


def scatter_about(rng, shape, scale, bound, split=(), held_as=jnp.bfloat16):
    values = scale * jax.random.normal(rng, shape, jnp.float32)
    if split:
        values = values * block_levels(rng, shape, split, -0.22, 0.18)
    return jnp.clip(values, -bound, bound).astype(held_as)


def setup_inputs(seed: int = 0) -> dict:
    keys = jax.random.split(jax.random.key(seed), 9)
    return {
        "hidden": scatter_about(keys[0], (SEQS, TOKENS, D), 1.0, 6.0, ((1, 64), (2, 4))),
        "doc_lengths": jax.vmap(lambda own: ragged_sizes(own, NDOC, TOKENS, MAXDOC, 2))(jax.random.split(keys[1], SEQS)).reshape((SEQS, NDOC)).astype(jnp.int32),
        "gain_se": jnp.clip(1.0 + 0.1 * jax.random.normal(keys[2], (D,), jnp.float32), 0.5, 1.5),
        "gain_mr": jnp.clip(1.0 + 0.1 * jax.random.normal(keys[3], (D,), jnp.float32), 0.5, 1.5),
        "feat_se": scatter_about(keys[4], (3, FEAT_TAPS, D), 0.6, 4.0, ((2, 4),), jnp.float32),
        "feat_mr": scatter_about(keys[5], (3, FEAT_TAPS, D), 0.6, 4.0, ((2, 4),), jnp.float32),
        "filter_se": scatter_about(keys[6], (GROUPS, SHORT_TAPS), 0.4, 3.0, ((0, 4),), jnp.float32),
        "filter_mr": scatter_about(keys[7], (GROUPS, MEDIUM_TAPS), MEDIUM_TAPS ** -0.5, 0.5, ((0, 4),)),
    }


norm_epsilon = 1e-06

def doc_offsets(doc_lengths, positions):
    doc_ends = jnp.cumsum(doc_lengths, axis=-1, dtype=jnp.int32)
    doc_starts = doc_ends - doc_lengths
    starts_before = doc_starts[:, None, :] <= positions[None, :, None]
    doc_first = lax.optimization_barrier(jnp.max(jnp.where(starts_before, doc_starts[:, None, :], 0), axis=-1))
    return (positions[None, :] - doc_first).astype(jnp.int32)

def delayed(inputs, shift_by):
    if shift_by == 0:
        return inputs
    zero_rows = jnp.zeros(inputs.shape[:1] + (shift_by,) + inputs.shape[2:], inputs.dtype)
    return jnp.concatenate([zero_rows, inputs[:, :inputs.shape[1] - shift_by]], axis=1)

def rms_normed(inputs, gain):
    mean_square = lax.optimization_barrier(jnp.sum(inputs * inputs, axis=-1)) / D
    return (inputs * lax.rsqrt(mean_square + norm_epsilon)[..., None] * gain).astype(jnp.bfloat16)

def featurize(normed, taps, offsets):
    inputs = normed.astype(jnp.float32)
    streams = []
    for stream_index in range(3):
        running = jnp.zeros(inputs.shape, jnp.float32)
        for tap_lag in range(FEAT_TAPS):
            keep_mask = (offsets >= tap_lag).astype(jnp.float32)[:, :, None]
            running = running + taps[stream_index, tap_lag] * delayed(inputs, tap_lag) * keep_mask
        streams.append(running)
    return streams

def short_conv(product, filters, offsets):
    per_channel = jnp.repeat(filters, product.shape[2] // filters.shape[0], axis=0)
    running = jnp.zeros(product.shape, jnp.float32)
    for tap_lag in range(SHORT_TAPS):
        keep_mask = (offsets >= tap_lag).astype(jnp.float32)[:, :, None]
        running = running + per_channel[:, tap_lag] * delayed(product, tap_lag) * keep_mask
    return running

def long_conv(mixed, filters, offsets):
    seq_count, seq_length, local_width = mixed.shape
    group_count = filters.shape[0]
    group_size = local_width // group_count
    block_rows = 128
    padded = jnp.concatenate([jnp.zeros((seq_count, MEDIUM_TAPS, local_width), mixed.dtype), mixed], axis=1)
    tap_lag = jnp.arange(block_rows, dtype=jnp.int32)[:, None] + MEDIUM_TAPS - jnp.arange(block_rows + MEDIUM_TAPS, dtype=jnp.int32)[None, :]
    in_range = (tap_lag >= 0) & (tap_lag < MEDIUM_TAPS)
    table = filters.astype(jnp.float32)[:, jnp.clip(tap_lag, 0, MEDIUM_TAPS - 1)]
    toeplitz = jnp.where(in_range[None], table, jnp.zeros((), jnp.float32))
    block_count = seq_length // block_rows

    def one_block(item_index):
        seq_index = item_index // block_count
        block_index = item_index % block_count
        window_rows = lax.dynamic_slice(padded, (seq_index, block_index * block_rows, jnp.int32(0)), (1, block_rows + MEDIUM_TAPS, local_width))[0]
        window_rows = window_rows.astype(jnp.float32).reshape(block_rows + MEDIUM_TAPS, group_count, group_size)
        block_offsets = lax.dynamic_slice(offsets, (seq_index, block_index * block_rows), (1, block_rows))[0]
        keep_mask = (tap_lag <= block_offsets[:, None]).astype(jnp.float32)
        masked_toep = toeplitz * keep_mask[None]
        convolved = jnp.einsum('gts,sgc->tgc', masked_toep, window_rows, precision=lax.Precision.HIGHEST)
        return convolved.reshape(block_rows, local_width)
    blocks = lax.map(one_block, jnp.arange(seq_count * block_count, dtype=jnp.int32))
    return blocks.reshape(seq_count, seq_length, local_width)

def one_sequence(packed):
    hidden_one, lengths_one = packed
    hidden_one = hidden_one[None]
    positions = jnp.arange(TOKENS, dtype=jnp.int32)
    offsets = doc_offsets(lengths_one[None], positions)
    return (hidden_one, offsets)

def reference(hidden, doc_lengths, gain_se, gain_mr, feat_se, feat_mr, filter_se, filter_mr):

    def per_sequence(packed):
        hidden_one, offsets = one_sequence(packed)
        stream_in = hidden_one.astype(jnp.float32)
        normed_one = rms_normed(stream_in, gain_se)
        query_one, key_one, value_one = featurize(normed_one, feat_se, offsets)
        middle = (stream_in + query_one * short_conv(key_one * value_one, filter_se, offsets)).astype(jnp.bfloat16)
        middle_f = middle.astype(jnp.float32)
        normed_two = rms_normed(middle_f, gain_mr)
        query_two, key_two, value_two = featurize(normed_two, feat_mr, offsets)
        mixed = (key_two * value_two).astype(jnp.bfloat16)
        medium = long_conv(mixed, filter_mr, offsets)
        return (middle_f + query_two * medium).astype(jnp.bfloat16)[0]
    return lax.map(per_sequence, (hidden, doc_lengths))
```

```python
import jax
import jax.numpy as jnp
from jax import lax
from jax.experimental import pallas as pl
from jax.experimental.pallas import tpu as pltpu
from jax.sharding import PartitionSpec as P

D = 8192
FEAT_TAPS = 3
SHORT_TAPS = 7
MEDIUM_TAPS = 128
HALO = 144
LANES = 128
GROUP = 16
CHUNK = 16
PAD = 8

norm_epsilon = 1e-06
VMEM_LIMIT = 48 * 1024 * 1024


def shifted(x, axis, by):
    peers = lax.axis_size(axis)
    pairs = [(i, i + by) for i in range(peers) if 0 <= i + by < peers]
    return lax.ppermute(x, axis, pairs)


def as_row(column):
    rows = column.shape[0]
    return jnp.broadcast_to(column, (rows, LANES)).T[0:1]


def as_column(row):
    return jnp.broadcast_to(row, (LANES, row.shape[1])).T


def sums_kernel(x_ref, s_ref):
    rows, width = x_ref.shape
    for r in range(0, rows, 64):
        total = jnp.zeros((64, LANES), jnp.float32)
        for c in range(0, width, LANES):
            x = x_ref[r : r + 64, c : c + LANES].astype(jnp.float32)
            total = total + x * x
        col = jnp.sum(total, axis=1, keepdims=True)
        if r % 128 == 0:
            held = col
        else:
            s_ref[0:1, r - 64 : r + 64] = as_row(jnp.concatenate([held, col], axis=0))


def prep_kernel(first_ref, len_ref, fse_ref, fmr_ref, off_ref, fexp_ref, base_ref, rev_ref):
    ext = off_ref.shape[0]
    width = fexp_ref.shape[1]
    groups = fmr_ref.shape[0]
    lens = jnp.broadcast_to(len_ref[0:1, :].astype(jnp.float32), (8, LANES))
    lane = lax.broadcasted_iota(jnp.int32, (8, LANES), 1)
    ends = lens
    step = 1
    while step < LANES:
        ends = ends + jnp.where(lane >= step, pltpu.roll(ends, step, 1), 0.0)
        step *= 2
    starts = (ends - lens)[0:1]
    first = first_ref[0] - HALO
    for r in range(0, ext, CHUNK):
        pos = (lax.broadcasted_iota(jnp.int32, (CHUNK, LANES), 0) + (first + r)).astype(jnp.float32)
        doc_first = jnp.max(jnp.where(starts <= pos, starts, 0.0), axis=1, keepdims=True)
        off_ref[r : r + CHUNK, :] = pos - doc_first
    fse = fse_ref[...]
    for c in range(0, width, LANES):
        row = lax.broadcasted_iota(jnp.int32, (groups, LANES), 0)
        col = lax.broadcasted_iota(jnp.int32, (groups, LANES), 1)
        spread = (row == (c + col) // GROUP).astype(jnp.float32)
        fexp_ref[:, c : c + LANES] = jnp.dot(
            fse, spread, preferred_element_type=jnp.float32, precision=lax.Precision.HIGHEST
        )
    row = lax.broadcasted_iota(jnp.int32, (LANES, LANES), 0)
    col = lax.broadcasted_iota(jnp.int32, (LANES, LANES), 1)
    flip = ((row + col) % MEDIUM_TAPS == 0).astype(jnp.bfloat16)
    rev_ref[...] = jnp.dot(fmr_ref[...], flip, preferred_element_type=jnp.float32)

    def one(g, carry):
        h = jnp.broadcast_to(rev_ref[pl.ds(g, 1), :], (GROUP, LANES))
        base_ref[g] = pltpu.roll(h, 0, 1, stride=1, stride_axis=0)
        return carry

    lax.fori_loop(0, groups, one, 0, unroll=8)


def scale_columns(sums_ref, scale_ref):
    tp = sums_ref.shape[0]
    total = sums_ref[0]
    for i in range(1, tp):
        total = total + sums_ref[i]
    scale = lax.rsqrt(total / D + norm_epsilon)
    own = scale.shape[1]
    scale_ref[0:HALO, :] = as_column(scale[0:1])[own - HALO :, :]
    scale_ref[HALO:, :] = as_column(scale[1:2])


def masks_of(off_ref, mask_ref, taps):
    for r in range(0, off_ref.shape[0], CHUNK):
        off = off_ref[r : r + CHUNK, :]
        for j in range(1, taps):
            mask_ref[j - 1, r : r + CHUNK, :] = (off >= j).astype(jnp.float32)


def se_kernel(
    x_ref, halo_ref, sums_ref, off_ref, gain_ref, feat_ref, fexp_ref, mid_ref, s_ref,
    scale_ref, mask_ref, norm_ref, prod_ref, q_ref, acc_ref,
):
    own, width = x_ref.shape
    ext = HALO + own
    scale_columns(sums_ref, scale_ref)
    masks_of(off_ref, mask_ref, SHORT_TAPS)
    norm_ref[0:PAD, :] = jnp.zeros((PAD, LANES), jnp.float32)
    prod_ref[0:PAD, :] = jnp.zeros((PAD, LANES), jnp.float32)
    acc_ref[...] = jnp.zeros(acc_ref.shape, jnp.float32)

    def raw(e, cols):
        if e < HALO:
            return halo_ref[e : e + CHUNK, cols].astype(jnp.float32)
        return x_ref[e - HALO : e - HALO + CHUNK, cols].astype(jnp.float32)

    def tile(i, carry):
        cols = pl.ds(pl.multiple_of(i * LANES, LANES), LANES)
        gain = gain_ref[0:1, cols]
        for e in range(0, ext, CHUNK):
            n = raw(e, cols) * scale_ref[e : e + CHUNK, :] * gain
            norm_ref[PAD + e : PAD + e + CHUNK, :] = n.astype(jnp.bfloat16).astype(jnp.float32)
        taps = [[feat_ref[s, j : j + 1, cols] for j in range(FEAT_TAPS)] for s in range(3)]
        for e in range(0, ext, CHUNK):
            xs = [norm_ref[PAD + e : PAD + e + CHUNK, :]]
            for j in range(1, FEAT_TAPS):
                xs.append(norm_ref[PAD + e - j : PAD + e - j + CHUNK, :] * mask_ref[j - 1, e : e + CHUNK, :])
            q, k, v = (
                taps[s][0] * xs[0] + taps[s][1] * xs[1] + taps[s][2] * xs[2] for s in range(3)
            )
            prod_ref[PAD + e : PAD + e + CHUNK, :] = k * v
            q_ref[e : e + CHUNK, :] = q
        filt = [fexp_ref[j : j + 1, cols] for j in range(SHORT_TAPS)]
        for e in range(0, ext, CHUNK):
            total = filt[0] * prod_ref[PAD + e : PAD + e + CHUNK, :]
            for j in range(1, SHORT_TAPS):
                total = total + filt[j] * (
                    prod_ref[PAD + e - j : PAD + e - j + CHUNK, :] * mask_ref[j - 1, e : e + CHUNK, :]
                )
            mid = (raw(e, cols) + q_ref[e : e + CHUNK, :] * total).astype(jnp.bfloat16)
            mid_ref[e : e + CHUNK, cols] = mid
            mid = mid.astype(jnp.float32)
            at = slice(own - HALO + e, own - HALO + e + CHUNK)
            acc_ref[at, :] = acc_ref[at, :] + mid * mid
        return carry

    lax.fori_loop(0, width // LANES, tile, 0)
    for part in range(2):
        for r in range(0, own, LANES):
            at = part * own + r
            col = jnp.sum(acc_ref[at : at + LANES, :], axis=1, keepdims=True)
            s_ref[part : part + 1, r : r + LANES] = as_row(col)


def mr_kernel(
    mid_ref, sums_ref, off_ref, gain_ref, feat_ref, base_ref, out_ref,
    scale_ref, mask_ref, norm_ref, mixed_ref, q_ref, keep_ref, toep_ref,
):
    ext, width = mid_ref.shape
    own = ext - HALO
    blocks = own // LANES
    per_tile = LANES // GROUP
    scale_columns(sums_ref, scale_ref)
    masks_of(off_ref, mask_ref, FEAT_TAPS)
    norm_ref[0:PAD, :] = jnp.zeros((PAD, LANES), jnp.float32)
    row = lax.broadcasted_iota(jnp.int32, (LANES, LANES), 0)
    col = lax.broadcasted_iota(jnp.int32, (LANES, LANES), 1)
    for b in range(blocks):
        off = off_ref[HALO + b * LANES : HALO + (b + 1) * LANES, :]
        lag = (row - col).astype(jnp.float32)
        before = (col > row) & (lag + MEDIUM_TAPS <= off)
        within = (row >= col) & (lag <= off)
        keep_ref[b, :, 0:LANES] = before.astype(jnp.float32).astype(jnp.bfloat16)
        keep_ref[b, :, LANES:] = within.astype(jnp.float32).astype(jnp.bfloat16)
    group_of = lax.broadcasted_iota(jnp.int32, (LANES, LANES), 1) // GROUP

    def tile(i, carry):
        cols = pl.ds(pl.multiple_of(i * LANES, LANES), LANES)
        gain = gain_ref[0:1, cols]
        for e in range(0, ext, CHUNK):
            n = mid_ref[e : e + CHUNK, cols].astype(jnp.float32) * scale_ref[e : e + CHUNK, :] * gain
            norm_ref[PAD + e : PAD + e + CHUNK, :] = n.astype(jnp.bfloat16).astype(jnp.float32)
        taps = [[feat_ref[s, j : j + 1, cols] for j in range(FEAT_TAPS)] for s in range(3)]
        for e in range(HALO - LANES, ext, CHUNK):
            xs = [norm_ref[PAD + e : PAD + e + CHUNK, :]]
            for j in range(1, FEAT_TAPS):
                xs.append(norm_ref[PAD + e - j : PAD + e - j + CHUNK, :] * mask_ref[j - 1, e : e + CHUNK, :])
            k, v = (taps[s][0] * xs[0] + taps[s][1] * xs[1] + taps[s][2] * xs[2] for s in (1, 2))
            w = e - (HALO - LANES)
            mixed_ref[w : w + CHUNK, :] = (k * v).astype(jnp.bfloat16)
            if e >= HALO:
                q = taps[0][0] * xs[0] + taps[0][1] * xs[1] + taps[0][2] * xs[2]
                q_ref[e - HALO : e - HALO + CHUNK, :] = q
        for g in range(per_tile):
            base = base_ref[i * per_tile + g]
            for r in range(0, LANES, GROUP):
                turned = (pltpu.roll(base, r, 1) if r else base).astype(jnp.bfloat16)
                for b in range(blocks):
                    at = slice(g * LANES + r, g * LANES + r + GROUP)
                    toep_ref[b, at, 0:LANES] = turned * keep_ref[b, r : r + GROUP, 0:LANES]
                    toep_ref[b, at, LANES:] = turned * keep_ref[b, r : r + GROUP, LANES:]
        for b in range(blocks):
            window = mixed_ref[b * LANES : (b + 2) * LANES, :]
            medium = jnp.zeros((LANES, LANES), jnp.float32)
            for g in range(per_tile):
                y = jnp.dot(
                    toep_ref[b, g * LANES : (g + 1) * LANES, :], window, preferred_element_type=jnp.float32
                )
                medium = y if g == 0 else jnp.where(group_of == g, y, medium)
            rows = slice(b * LANES, (b + 1) * LANES)
            mid = mid_ref[HALO + b * LANES : HALO + (b + 1) * LANES, cols].astype(jnp.float32)
            out_ref[rows, cols] = (mid + q_ref[rows, :] * medium).astype(jnp.bfloat16)
        return carry

    lax.fori_loop(0, width // LANES, tile, 0)


def call(kernel, out_shape, scratch, flops, nbytes, smem=0):
    count = smem
    params = pltpu.CompilerParams(vmem_limit_bytes=VMEM_LIMIT)
    cost = pl.CostEstimate(flops=flops, bytes_accessed=nbytes, transcendentals=0)

    def run(*operands):
        specs = [pl.BlockSpec(memory_space=pltpu.SMEM)] * count
        specs += [pl.BlockSpec(memory_space=pltpu.VMEM)] * (len(operands) - count)
        return pl.pallas_call(
            kernel, out_shape=out_shape, in_specs=specs,
            out_specs=jax.tree.map(lambda _: pl.BlockSpec(memory_space=pltpu.VMEM), out_shape),
            scratch_shapes=scratch, compiler_params=params, cost_estimate=cost,
        )(*operands)

    return run


def shards(hidden, doc_lengths, gain_se, gain_mr, feat_se, feat_mr, filter_se, filter_mr):
    f32, bf16 = jnp.float32, jnp.bfloat16
    shape = jax.ShapeDtypeStruct
    own, width = hidden.shape[1:]
    ext = HALO + own
    groups = filter_se.shape[0]
    x = hidden[0]
    first = (lax.axis_index("ctx") * own).astype(jnp.int32).reshape(1)
    part = call(sums_kernel, shape((1, own), f32), [], 1 << 20, 1 << 20)(x)
    before = shifted(part, "ctx", 1)
    halo = shifted(x[own - HALO :], "ctx", 1)
    off, fexp, base = call(
        prep_kernel,
        (shape((ext, LANES), f32), shape((8, width), f32), shape((groups, GROUP, LANES), f32)),
        [pltpu.VMEM((groups, LANES), f32)], 1 << 24, 1 << 20, smem=1,
    )(first, doc_lengths, jnp.pad(filter_se.T, ((0, 1), (0, 0))), filter_mr)
    sums = lax.all_gather(jnp.concatenate([before, part], axis=0), "tp")
    mid, part_two = call(
        se_kernel,
        (shape((ext, width), bf16), shape((2, own), f32)),
        [
            pltpu.VMEM((ext, LANES), f32),
            pltpu.VMEM((SHORT_TAPS - 1, ext, LANES), f32),
            pltpu.VMEM((PAD + ext, LANES), f32),
            pltpu.VMEM((PAD + ext, LANES), f32),
            pltpu.VMEM((ext, LANES), f32),
            pltpu.VMEM((2 * own, LANES), f32),
        ],
        50 << 20, 4 << 20,
    )(x, halo, sums, off, gain_se.reshape(1, width), feat_se, fexp)
    sums_two = lax.all_gather(part_two, "tp")
    out = call(
        mr_kernel,
        shape((own, width), bf16),
        [
            pltpu.VMEM((ext, LANES), f32),
            pltpu.VMEM((FEAT_TAPS - 1, ext, LANES), f32),
            pltpu.VMEM((PAD + ext, LANES), f32),
            pltpu.VMEM((own + LANES, LANES), bf16),
            pltpu.VMEM((own, LANES), f32),
            pltpu.VMEM((own // LANES, LANES, 2 * LANES), bf16),
            pltpu.VMEM((own // LANES, (LANES // GROUP) * LANES, 2 * LANES), bf16),
        ],
        1 << 30, 4 << 20,
    )(mid, sums_two, off, gain_mr.reshape(1, width), feat_mr, base)
    return out[None]


def solution(mesh):
    in_specs = (
        P(None, "ctx", "tp"),
        P(),
        P("tp"),
        P("tp"),
        P(None, None, "tp"),
        P(None, None, "tp"),
        P("tp", None),
        P("tp", None),
    )
    out_specs = P(None, "ctx", "tp")
    return jax.shard_map(shards, mesh=mesh, in_specs=in_specs, out_specs=out_specs, check_vma=False)
```

```python
import jax
import jax.numpy as jnp
from jax import lax
from jax.experimental import pallas as pl
from jax.experimental.pallas import tpu as pltpu
from jax.sharding import PartitionSpec as P

D = 8192
FEAT_TAPS = 3
SHORT_TAPS = 7
MEDIUM_TAPS = 128
HALO = 144
LANES = 128
GROUP = 16
CHUNK = 16
PAD = 8

norm_epsilon = 1e-06
VMEM_LIMIT = 48 * 1024 * 1024


def shifted(x, axis, by):
    peers = lax.axis_size(axis)
    pairs = [(i, i + by) for i in range(peers) if 0 <= i + by < peers]
    return lax.ppermute(x, axis, pairs)


def as_row(column):
    rows = column.shape[0]
    return jnp.broadcast_to(column, (rows, LANES)).T[0:1]


def as_column(row):
    return jnp.broadcast_to(row, (LANES, row.shape[1])).T


def sums_kernel(x_ref, s_ref):
    rows, width = x_ref.shape
    for r in range(0, rows, 64):
        total = jnp.zeros((64, LANES), jnp.float32)
        for c in range(0, width, LANES):
            x = x_ref[r : r + 64, c : c + LANES].astype(jnp.float32)
            total = total + x * x
        col = jnp.sum(total, axis=1, keepdims=True)
        if r % 128 == 0:
            held = col
        else:
            s_ref[0:1, r - 64 : r + 64] = as_row(jnp.concatenate([held, col], axis=0))


def prep_kernel(first_ref, x_ref, len_ref, fse_ref, fmr_ref, off_ref, fexp_ref, base_ref, last_ref, rev_ref):
    last_ref[...] = x_ref[x_ref.shape[0] - HALO :, :]
    ext = off_ref.shape[0]
    width = fexp_ref.shape[1]
    groups = fmr_ref.shape[0]
    lens = jnp.broadcast_to(len_ref[0:1, :].astype(jnp.float32), (8, LANES))
    lane = lax.broadcasted_iota(jnp.int32, (8, LANES), 1)
    ends = lens
    step = 1
    while step < LANES:
        ends = ends + jnp.where(lane >= step, pltpu.roll(ends, step, 1), 0.0)
        step *= 2
    starts = (ends - lens)[0:1]
    first = first_ref[0] - HALO
    for r in range(0, ext, CHUNK):
        pos = (lax.broadcasted_iota(jnp.int32, (CHUNK, LANES), 0) + (first + r)).astype(jnp.float32)
        doc_first = jnp.max(jnp.where(starts <= pos, starts, 0.0), axis=1, keepdims=True)
        off_ref[r : r + CHUNK, :] = pos - doc_first
    fse = fse_ref[...]
    for c in range(0, width, LANES):
        row = lax.broadcasted_iota(jnp.int32, (groups, LANES), 0)
        col = lax.broadcasted_iota(jnp.int32, (groups, LANES), 1)
        spread = (row == (c + col) // GROUP).astype(jnp.float32)
        fexp_ref[:, c : c + LANES] = jnp.dot(
            fse, spread, preferred_element_type=jnp.float32, precision=lax.Precision.HIGHEST
        )
    row = lax.broadcasted_iota(jnp.int32, (LANES, LANES), 0)
    col = lax.broadcasted_iota(jnp.int32, (LANES, LANES), 1)
    flip = ((row + col) % MEDIUM_TAPS == 0).astype(jnp.bfloat16)
    rev_ref[...] = jnp.dot(fmr_ref[...], flip, preferred_element_type=jnp.float32)

    def one(g, carry):
        h = jnp.broadcast_to(rev_ref[pl.ds(g, 1), :], (GROUP, LANES))
        base_ref[g] = pltpu.roll(h, 0, 1, stride=1, stride_axis=0)
        return carry

    lax.fori_loop(0, groups, one, 0, unroll=8)


def scale_columns(sums_ref, scale_ref):
    tp = sums_ref.shape[0]
    total = sums_ref[0]
    for i in range(1, tp):
        total = total + sums_ref[i]
    scale = lax.rsqrt(total / D + norm_epsilon)
    own = scale.shape[1]
    scale_ref[0:HALO, :] = as_column(scale[0:1])[own - HALO :, :]
    scale_ref[HALO:, :] = as_column(scale[1:2])


def masks_of(off_ref, mask_ref, taps):
    for r in range(0, off_ref.shape[0], CHUNK):
        off = off_ref[r : r + CHUNK, :]
        for j in range(1, taps):
            mask_ref[j - 1, r : r + CHUNK, :] = (off >= j).astype(jnp.float32)


def se_kernel(
    x_ref, halo_ref, sums_ref, off_ref, gain_ref, feat_ref, fexp_ref, mid_ref, s_ref,
    scale_ref, mask_ref, norm_ref, prod_ref, q_ref, acc_ref,
):
    own, width = x_ref.shape
    ext = HALO + own
    scale_columns(sums_ref, scale_ref)
    masks_of(off_ref, mask_ref, SHORT_TAPS)
    norm_ref[0:PAD, :] = jnp.zeros((PAD, LANES), jnp.float32)
    prod_ref[0:PAD, :] = jnp.zeros((PAD, LANES), jnp.float32)
    acc_ref[...] = jnp.zeros(acc_ref.shape, jnp.float32)

    def raw(e, cols):
        if e < HALO:
            return halo_ref[e : e + CHUNK, cols].astype(jnp.float32)
        return x_ref[e - HALO : e - HALO + CHUNK, cols].astype(jnp.float32)

    def tile(i, carry):
        cols = pl.ds(pl.multiple_of(i * LANES, LANES), LANES)
        gain = gain_ref[0:1, cols]
        for e in range(0, ext, CHUNK):
            n = raw(e, cols) * scale_ref[e : e + CHUNK, :] * gain
            norm_ref[PAD + e : PAD + e + CHUNK, :] = n.astype(jnp.bfloat16).astype(jnp.float32)
        taps = [[feat_ref[s, j : j + 1, cols] for j in range(FEAT_TAPS)] for s in range(3)]
        for e in range(0, ext, CHUNK):
            xs = [norm_ref[PAD + e : PAD + e + CHUNK, :]]
            for j in range(1, FEAT_TAPS):
                xs.append(norm_ref[PAD + e - j : PAD + e - j + CHUNK, :] * mask_ref[j - 1, e : e + CHUNK, :])
            q, k, v = (
                taps[s][0] * xs[0] + taps[s][1] * xs[1] + taps[s][2] * xs[2] for s in range(3)
            )
            prod_ref[PAD + e : PAD + e + CHUNK, :] = k * v
            q_ref[e : e + CHUNK, :] = q
        filt = [fexp_ref[j : j + 1, cols] for j in range(SHORT_TAPS)]
        for e in range(0, ext, CHUNK):
            total = filt[0] * prod_ref[PAD + e : PAD + e + CHUNK, :]
            for j in range(1, SHORT_TAPS):
                total = total + filt[j] * (
                    prod_ref[PAD + e - j : PAD + e - j + CHUNK, :] * mask_ref[j - 1, e : e + CHUNK, :]
                )
            mid = (raw(e, cols) + q_ref[e : e + CHUNK, :] * total).astype(jnp.bfloat16)
            mid_ref[e : e + CHUNK, cols] = mid
            mid = mid.astype(jnp.float32)
            at = slice(own - HALO + e, own - HALO + e + CHUNK)
            acc_ref[at, :] = acc_ref[at, :] + mid * mid
        return carry

    lax.fori_loop(0, width // LANES, tile, 0)
    for part in range(2):
        for r in range(0, own, LANES):
            at = part * own + r
            col = jnp.sum(acc_ref[at : at + LANES, :], axis=1, keepdims=True)
            s_ref[part : part + 1, r : r + LANES] = as_row(col)


def mr_kernel(
    mid_ref, sums_ref, off_ref, gain_ref, feat_ref, base_ref, out_ref,
    scale_ref, mask_ref, norm_ref, mixed_ref, q_ref, keep_ref, toep_ref,
):
    ext, width = mid_ref.shape
    own = ext - HALO
    blocks = own // LANES
    per_tile = LANES // GROUP
    scale_columns(sums_ref, scale_ref)
    masks_of(off_ref, mask_ref, FEAT_TAPS)
    norm_ref[0:PAD, :] = jnp.zeros((PAD, LANES), jnp.float32)
    row = lax.broadcasted_iota(jnp.int32, (LANES, LANES), 0)
    col = lax.broadcasted_iota(jnp.int32, (LANES, LANES), 1)
    for b in range(blocks):
        off = off_ref[HALO + b * LANES : HALO + (b + 1) * LANES, :]
        lag = (row - col).astype(jnp.float32)
        before = (col > row) & (lag + MEDIUM_TAPS <= off)
        within = (row >= col) & (lag <= off)
        keep_ref[b, :, 0:LANES] = before.astype(jnp.float32).astype(jnp.bfloat16)
        keep_ref[b, :, LANES:] = within.astype(jnp.float32).astype(jnp.bfloat16)
    group_of = lax.broadcasted_iota(jnp.int32, (LANES, LANES), 1) // GROUP

    def tile(i, carry):
        cols = pl.ds(pl.multiple_of(i * LANES, LANES), LANES)
        gain = gain_ref[0:1, cols]
        for e in range(0, ext, CHUNK):
            n = mid_ref[e : e + CHUNK, cols].astype(jnp.float32) * scale_ref[e : e + CHUNK, :] * gain
            norm_ref[PAD + e : PAD + e + CHUNK, :] = n.astype(jnp.bfloat16).astype(jnp.float32)
        taps = [[feat_ref[s, j : j + 1, cols] for j in range(FEAT_TAPS)] for s in range(3)]
        for e in range(HALO - LANES, ext, CHUNK):
            xs = [norm_ref[PAD + e : PAD + e + CHUNK, :]]
            for j in range(1, FEAT_TAPS):
                xs.append(norm_ref[PAD + e - j : PAD + e - j + CHUNK, :] * mask_ref[j - 1, e : e + CHUNK, :])
            k, v = (taps[s][0] * xs[0] + taps[s][1] * xs[1] + taps[s][2] * xs[2] for s in (1, 2))
            w = e - (HALO - LANES)
            mixed_ref[w : w + CHUNK, :] = (k * v).astype(jnp.bfloat16)
            if e >= HALO:
                q = taps[0][0] * xs[0] + taps[0][1] * xs[1] + taps[0][2] * xs[2]
                q_ref[e - HALO : e - HALO + CHUNK, :] = q
        for g in range(per_tile):
            base = base_ref[i * per_tile + g]
            for r in range(0, LANES, GROUP):
                turned = (pltpu.roll(base, r, 1) if r else base).astype(jnp.bfloat16)
                for b in range(blocks):
                    at = slice(g * LANES + r, g * LANES + r + GROUP)
                    toep_ref[b, at, 0:LANES] = turned * keep_ref[b, r : r + GROUP, 0:LANES]
                    toep_ref[b, at, LANES:] = turned * keep_ref[b, r : r + GROUP, LANES:]
        for b in range(blocks):
            window = mixed_ref[b * LANES : (b + 2) * LANES, :]
            y = jnp.dot(toep_ref[b], window, preferred_element_type=jnp.float32)
            medium = y[0:LANES]
            for g in range(1, per_tile):
                medium = jnp.where(group_of == g, y[g * LANES : (g + 1) * LANES], medium)
            rows = slice(b * LANES, (b + 1) * LANES)
            mid = mid_ref[HALO + b * LANES : HALO + (b + 1) * LANES, cols].astype(jnp.float32)
            out_ref[rows, cols] = (mid + q_ref[rows, :] * medium).astype(jnp.bfloat16)
        return carry

    lax.fori_loop(0, width // LANES, tile, 0)


def call(kernel, out_shape, scratch, flops, nbytes, smem=0):
    count = smem
    params = pltpu.CompilerParams(vmem_limit_bytes=VMEM_LIMIT)
    cost = pl.CostEstimate(flops=flops, bytes_accessed=nbytes, transcendentals=0)

    def run(*operands):
        specs = [pl.BlockSpec(memory_space=pltpu.SMEM)] * count
        specs += [pl.BlockSpec(memory_space=pltpu.VMEM)] * (len(operands) - count)
        return pl.pallas_call(
            kernel, out_shape=out_shape, in_specs=specs,
            out_specs=jax.tree.map(lambda _: pl.BlockSpec(memory_space=pltpu.VMEM), out_shape),
            scratch_shapes=scratch, compiler_params=params, cost_estimate=cost,
        )(*operands)

    return run


def se_call(x, halo, sums, off, gain, feat, fexp):
    own, width = x.shape
    ext = HALO + own
    return call(
        se_kernel,
        (jax.ShapeDtypeStruct((ext, width), jnp.bfloat16), jax.ShapeDtypeStruct((2, own), jnp.float32)),
        [
            pltpu.VMEM((ext, LANES), jnp.float32),
            pltpu.VMEM((SHORT_TAPS - 1, ext, LANES), jnp.float32),
            pltpu.VMEM((PAD + ext, LANES), jnp.float32),
            pltpu.VMEM((PAD + ext, LANES), jnp.float32),
            pltpu.VMEM((ext, LANES), jnp.float32),
            pltpu.VMEM((2 * own, LANES), jnp.float32),
        ],
        50 << 20, 4 << 20,
    )(x, halo, sums, off, gain, feat, fexp)


def mr_call(mid, sums, off, gain, feat, base):
    ext, width = mid.shape
    own = ext - HALO
    return call(
        mr_kernel,
        jax.ShapeDtypeStruct((own, width), jnp.bfloat16),
        [
            pltpu.VMEM((ext, LANES), jnp.float32),
            pltpu.VMEM((FEAT_TAPS - 1, ext, LANES), jnp.float32),
            pltpu.VMEM((PAD + ext, LANES), jnp.float32),
            pltpu.VMEM((own + LANES, LANES), jnp.bfloat16),
            pltpu.VMEM((own, LANES), jnp.float32),
            pltpu.VMEM((own // LANES, LANES, 2 * LANES), jnp.bfloat16),
            pltpu.VMEM((own // LANES, (LANES // GROUP) * LANES, 2 * LANES), jnp.bfloat16),
        ],
        1 << 30, 4 << 20,
    )(mid, sums, off, gain, feat, base)


def shards(hidden, doc_lengths, gain_se, gain_mr, feat_se, feat_mr, filter_se, filter_mr):
    f32, bf16 = jnp.float32, jnp.bfloat16
    shape = jax.ShapeDtypeStruct
    own, width = hidden.shape[1:]
    ext = HALO + own
    groups = filter_se.shape[0]
    x = hidden[0]
    first = (lax.axis_index("ctx") * own).astype(jnp.int32).reshape(1)
    part = call(sums_kernel, shape((1, own), f32), [], 1 << 20, 1 << 20)(x)
    before = shifted(part, "ctx", 1)
    off, fexp, base, last = call(
        prep_kernel,
        (
            shape((ext, LANES), f32),
            shape((8, width), f32),
            shape((groups, GROUP, LANES), f32),
            shape((HALO, width), bf16),
        ),
        [pltpu.VMEM((groups, LANES), f32)], 1 << 24, 1 << 20, smem=1,
    )(first, x, doc_lengths, jnp.pad(filter_se.T, ((0, 1), (0, 0))), filter_mr)
    halo = shifted(last, "ctx", 1)
    sums = lax.all_gather(jnp.concatenate([before, part], axis=0), "tp")
    mid, part_two = se_call(x, halo, sums, off, gain_se.reshape(1, width), feat_se, fexp)
    sums_two = lax.all_gather(part_two, "tp")
    out = mr_call(mid, sums_two, off, gain_mr.reshape(1, width), feat_mr, base)
    return out[None]


def solution(mesh):
    in_specs = (
        P(None, "ctx", "tp"),
        P(),
        P("tp"),
        P("tp"),
        P(None, None, "tp"),
        P(None, None, "tp"),
        P("tp", None),
        P("tp", None),
    )
    out_specs = P(None, "ctx", "tp")
    return jax.shard_map(shards, mesh=mesh, in_specs=in_specs, out_specs=out_specs, check_vma=False)
```

```python
import jax
import jax.numpy as jnp
from jax import lax
from jax.experimental import pallas as pl
from jax.experimental.pallas import tpu as pltpu
from jax.sharding import PartitionSpec as P

D = 8192
FEAT_TAPS = 3
SHORT_TAPS = 7
MEDIUM_TAPS = 128
HALO = 144
LANES = 128
GROUP = 16
CHUNK = 16
PAD = 8

norm_epsilon = 1e-06
VMEM_LIMIT = 48 * 1024 * 1024


def shifted(x, axis, by):
    peers = lax.axis_size(axis)
    pairs = [(i, i + by) for i in range(peers) if 0 <= i + by < peers]
    return lax.ppermute(x, axis, pairs)


def as_row(column):
    rows = column.shape[0]
    return jnp.broadcast_to(column, (rows, LANES)).T[0:1]


def as_column(row):
    return jnp.broadcast_to(row, (LANES, row.shape[1])).T


def sums_kernel(x_ref, s_ref):
    rows, width = x_ref.shape
    for r in range(0, rows, 64):
        total = jnp.zeros((64, LANES), jnp.float32)
        for c in range(0, width, LANES):
            x = x_ref[r : r + 64, c : c + LANES].astype(jnp.float32)
            total = total + x * x
        col = jnp.sum(total, axis=1, keepdims=True)
        if r % 128 == 0:
            held = col
        else:
            s_ref[0:1, r - 64 : r + 64] = as_row(jnp.concatenate([held, col], axis=0))


def place_kernel(first_ref, after_ref, len_ref, fse_ref, off_ref, fexp_ref):
    ext = off_ref.shape[0]
    width = fexp_ref.shape[1]
    groups = fse_ref.shape[0]
    lens = jnp.broadcast_to(len_ref[0:1, :].astype(jnp.float32), (8, LANES))
    lane = lax.broadcasted_iota(jnp.int32, (8, LANES), 1)
    ends = lens
    step = 1
    while step < LANES:
        ends = ends + jnp.where(lane >= step, pltpu.roll(ends, step, 1), 0.0)
        step *= 2
    starts = (ends - lens)[0:1]
    first = first_ref[0] - HALO
    for r in range(0, ext, CHUNK):
        pos = (lax.broadcasted_iota(jnp.int32, (CHUNK, LANES), 0) + (first + r)).astype(jnp.float32)
        doc_first = jnp.max(jnp.where(starts <= pos, starts, 0.0), axis=1, keepdims=True)
        off_ref[r : r + CHUNK, :] = pos - doc_first
    fse = fse_ref[...]
    for c in range(0, width, LANES):
        row = lax.broadcasted_iota(jnp.int32, (groups, LANES), 0)
        col = lax.broadcasted_iota(jnp.int32, (groups, LANES), 1)
        spread = (row == (c + col) // GROUP).astype(jnp.float32)
        fexp_ref[0:SHORT_TAPS, c : c + LANES] = lax.dot_general(
            fse, spread, (((0,), (0,)), ((), ())),
            preferred_element_type=jnp.float32, precision=lax.Precision.HIGHEST,
        )


def turn_kernel(after_ref, fmr_ref, base_ref, rev_ref):
    groups = fmr_ref.shape[0]
    row = lax.broadcasted_iota(jnp.int32, (LANES, LANES), 0)
    col = lax.broadcasted_iota(jnp.int32, (LANES, LANES), 1)
    flip = ((row + col) % MEDIUM_TAPS == 0).astype(jnp.bfloat16)
    rev_ref[...] = jnp.dot(fmr_ref[...], flip, preferred_element_type=jnp.float32)

    def one(g, carry):
        h = jnp.broadcast_to(rev_ref[pl.ds(g, 1), :], (GROUP, LANES))
        base_ref[g] = pltpu.roll(h, 0, 1, stride=1, stride_axis=0)
        return carry

    lax.fori_loop(0, groups, one, 0, unroll=8)


def scale_of(total):
    return lax.rsqrt(total / D + norm_epsilon)


def scale_columns(sums_ref, scale_ref):
    tp = sums_ref.shape[0]
    total = sums_ref[0]
    for i in range(1, tp):
        total = total + sums_ref[i]
    scale = scale_of(total)
    own = scale.shape[1]
    scale_ref[0:HALO, :] = as_column(scale[0:1])[own - HALO :, :]
    scale_ref[HALO:, :] = as_column(scale[1:2])


def masks_of(off_ref, mask_ref, taps, first=0):
    for r in range(0, mask_ref.shape[1], CHUNK):
        off = off_ref[first + r : first + r + CHUNK, :]
        for j in range(1, taps):
            mask_ref[j - 1, r : r + CHUNK, :] = (off >= j).astype(jnp.float32)


def se_rows(
    raw, rows, skip, width, gain_ref, feat_ref, fexp_ref, mid_ref,
    scale_ref, mask_ref, norm_ref, prod_ref, q_ref, acc_ref,
):
    norm_ref[0:PAD, :] = jnp.zeros((PAD, LANES), jnp.float32)
    prod_ref[0:PAD, :] = jnp.zeros((PAD, LANES), jnp.float32)
    acc_ref[...] = jnp.zeros(acc_ref.shape, jnp.float32)

    def tile(i, carry):
        cols = pl.ds(pl.multiple_of(i * LANES, LANES), LANES)
        gain = gain_ref[0:1, cols]
        for e in range(0, rows, CHUNK):
            n = raw(e, cols) * scale_ref[e : e + CHUNK, :] * gain
            norm_ref[PAD + e : PAD + e + CHUNK, :] = n.astype(jnp.bfloat16).astype(jnp.float32)
        taps = [[feat_ref[s, j : j + 1, cols] for j in range(FEAT_TAPS)] for s in range(3)]
        for e in range(0, rows, CHUNK):
            xs = [norm_ref[PAD + e : PAD + e + CHUNK, :]]
            for j in range(1, FEAT_TAPS):
                xs.append(norm_ref[PAD + e - j : PAD + e - j + CHUNK, :] * mask_ref[j - 1, e : e + CHUNK, :])
            q, k, v = (
                taps[s][0] * xs[0] + taps[s][1] * xs[1] + taps[s][2] * xs[2] for s in range(3)
            )
            prod_ref[PAD + e : PAD + e + CHUNK, :] = k * v
            q_ref[e : e + CHUNK, :] = q
        filt = [fexp_ref[j : j + 1, cols] for j in range(SHORT_TAPS)]
        for e in range(skip, rows, CHUNK):
            total = filt[0] * prod_ref[PAD + e : PAD + e + CHUNK, :]
            for j in range(1, SHORT_TAPS):
                total = total + filt[j] * (
                    prod_ref[PAD + e - j : PAD + e - j + CHUNK, :] * mask_ref[j - 1, e : e + CHUNK, :]
                )
            mid = (raw(e, cols) + q_ref[e : e + CHUNK, :] * total).astype(jnp.bfloat16)
            mid_ref[e : e + CHUNK, cols] = mid
            mid = mid.astype(jnp.float32)
            acc_ref[e : e + CHUNK, :] = acc_ref[e : e + CHUNK, :] + mid * mid
        return carry

    lax.fori_loop(0, width // LANES, tile, 0)


def se_own_kernel(
    x_ref, total_ref, off_ref, gain_ref, feat_ref, fexp_ref, mid_ref, s_ref, scale_ref, mask_ref, *scratch,
):
    own, width = x_ref.shape
    acc_ref = scratch[-1]
    scale_ref[...] = as_column(scale_of(total_ref[...]))
    masks_of(off_ref, mask_ref, SHORT_TAPS, HALO)
    mid_ref[0:CHUNK, :] = jnp.zeros((CHUNK, width), jnp.bfloat16)
    se_rows(
        lambda e, cols: x_ref[e : e + CHUNK, cols].astype(jnp.float32),
        own, CHUNK, width, gain_ref, feat_ref, fexp_ref, mid_ref, scale_ref, mask_ref, *scratch,
    )
    for r in range(0, own, LANES):
        s_ref[0:1, r : r + LANES] = as_row(jnp.sum(acc_ref[r : r + LANES, :], axis=1, keepdims=True))


def se_halo_kernel(
    x_ref, halo_ref, total_ref, before_ref, part_ref, off_ref, gain_ref, feat_ref, fexp_ref, mid_ref, s_ref,
    scale_ref, mask_ref, *scratch,
):
    own, width = x_ref.shape
    acc_ref = scratch[-1]
    scale_ref[0:HALO, :] = as_column(scale_of(before_ref[...]))[own - HALO :, :]
    scale_ref[HALO:, :] = as_column(scale_of(total_ref[...]))[0:CHUNK, :]
    masks_of(off_ref, mask_ref, SHORT_TAPS)

    def raw(e, cols):
        if e < HALO:
            return halo_ref[e : e + CHUNK, cols].astype(jnp.float32)
        return x_ref[e - HALO : e - HALO + CHUNK, cols].astype(jnp.float32)

    se_rows(
        raw, HALO + CHUNK, 0, width, gain_ref, feat_ref, fexp_ref, mid_ref, scale_ref, mask_ref, *scratch
    )
    halo_part = jnp.sum(acc_ref[0:HALO, :], axis=1, keepdims=True)
    halo_part = jnp.concatenate([jnp.zeros((own - HALO, 1), jnp.float32), halo_part], axis=0)
    own_part = jnp.sum(acc_ref[HALO:, :], axis=1, keepdims=True)
    own_part = jnp.concatenate([own_part, jnp.zeros((own - CHUNK, 1), jnp.float32)], axis=0)
    s_ref[0:1, :] = as_row(halo_part)
    s_ref[1:2, :] = as_row(own_part) + part_ref[...]


def mr_kernel(
    early_ref, mid_ref, sums_ref, off_ref, gain_ref, feat_ref, base_ref, out_ref,
    scale_ref, mask_ref, norm_ref, mixed_ref, q_ref, keep_ref, toep_ref,
):
    own, width = mid_ref.shape
    ext = HALO + own
    blocks = own // LANES
    per_tile = LANES // GROUP
    scale_columns(sums_ref, scale_ref)
    masks_of(off_ref, mask_ref, FEAT_TAPS)
    norm_ref[0:PAD, :] = jnp.zeros((PAD, LANES), jnp.float32)
    row = lax.broadcasted_iota(jnp.int32, (LANES, LANES), 0)
    col = lax.broadcasted_iota(jnp.int32, (LANES, LANES), 1)
    for b in range(blocks):
        off = off_ref[HALO + b * LANES : HALO + (b + 1) * LANES, :]
        lag = (row - col).astype(jnp.float32)
        before = (col > row) & (lag + MEDIUM_TAPS <= off)
        within = (row >= col) & (lag <= off)
        keep_ref[b, :, 0:LANES] = before.astype(jnp.float32).astype(jnp.bfloat16)
        keep_ref[b, :, LANES:] = within.astype(jnp.float32).astype(jnp.bfloat16)
    early = early_ref.shape[0]

    def middle(e, cols):
        held = early_ref[e : e + CHUNK, cols] if e < early else mid_ref[e - HALO : e - HALO + CHUNK, cols]
        return held.astype(jnp.float32)

    group_of = lax.broadcasted_iota(jnp.int32, (LANES, LANES), 1) // GROUP

    def tile(i, carry):
        cols = pl.ds(pl.multiple_of(i * LANES, LANES), LANES)
        gain = gain_ref[0:1, cols]
        for e in range(0, ext, CHUNK):
            n = middle(e, cols) * scale_ref[e : e + CHUNK, :] * gain
            norm_ref[PAD + e : PAD + e + CHUNK, :] = n.astype(jnp.bfloat16).astype(jnp.float32)
        taps = [[feat_ref[s, j : j + 1, cols] for j in range(FEAT_TAPS)] for s in range(3)]
        for e in range(HALO - LANES, ext, CHUNK):
            xs = [norm_ref[PAD + e : PAD + e + CHUNK, :]]
            for j in range(1, FEAT_TAPS):
                xs.append(norm_ref[PAD + e - j : PAD + e - j + CHUNK, :] * mask_ref[j - 1, e : e + CHUNK, :])
            k, v = (taps[s][0] * xs[0] + taps[s][1] * xs[1] + taps[s][2] * xs[2] for s in (1, 2))
            w = e - (HALO - LANES)
            mixed_ref[w : w + CHUNK, :] = (k * v).astype(jnp.bfloat16)
            if e >= HALO:
                q = taps[0][0] * xs[0] + taps[0][1] * xs[1] + taps[0][2] * xs[2]
                q_ref[e - HALO : e - HALO + CHUNK, :] = q
        for g in range(per_tile):
            base = base_ref[i * per_tile + g]
            for r in range(0, LANES, GROUP):
                turned = (pltpu.roll(base, r, 1) if r else base).astype(jnp.bfloat16)
                for b in range(blocks):
                    at = slice(g * LANES + r, g * LANES + r + GROUP)
                    toep_ref[b, at, 0:LANES] = turned * keep_ref[b, r : r + GROUP, 0:LANES]
                    toep_ref[b, at, LANES:] = turned * keep_ref[b, r : r + GROUP, LANES:]
        for b in range(blocks):
            window = mixed_ref[b * LANES : (b + 2) * LANES, :]
            y = jnp.dot(toep_ref[b], window, preferred_element_type=jnp.float32)
            medium = y[0:LANES]
            for g in range(1, per_tile):
                medium = jnp.where(group_of == g, y[g * LANES : (g + 1) * LANES], medium)
            for r in range(0, LANES, CHUNK):
                t = b * LANES + r
                out = middle(HALO + t, cols) + q_ref[t : t + CHUNK, :] * medium[r : r + CHUNK]
                out_ref[t : t + CHUNK, cols] = out.astype(jnp.bfloat16)
        return carry

    lax.fori_loop(0, width // LANES, tile, 0)


def call(kernel, out_shape, scratch, flops, nbytes, smem=0):
    count = smem
    params = pltpu.CompilerParams(vmem_limit_bytes=VMEM_LIMIT)
    cost = pl.CostEstimate(flops=flops, bytes_accessed=nbytes, transcendentals=0)

    def run(*operands):
        specs = [pl.BlockSpec(memory_space=pltpu.SMEM)] * count
        specs += [pl.BlockSpec(memory_space=pltpu.VMEM)] * (len(operands) - count)
        return pl.pallas_call(
            kernel, out_shape=out_shape, in_specs=specs,
            out_specs=jax.tree.map(lambda _: pl.BlockSpec(memory_space=pltpu.VMEM), out_shape),
            scratch_shapes=scratch, compiler_params=params, cost_estimate=cost,
        )(*operands)

    return run


def se_scratch(rows):
    return [
        pltpu.VMEM((rows, LANES), jnp.float32),
        pltpu.VMEM((SHORT_TAPS - 1, rows, LANES), jnp.float32),
        pltpu.VMEM((PAD + rows, LANES), jnp.float32),
        pltpu.VMEM((PAD + rows, LANES), jnp.float32),
        pltpu.VMEM((rows, LANES), jnp.float32),
        pltpu.VMEM((rows, LANES), jnp.float32),
    ]


def se_own_call(x, *rest):
    own, width = x.shape
    shapes = (jax.ShapeDtypeStruct((own, width), jnp.bfloat16), jax.ShapeDtypeStruct((1, own), jnp.float32))
    return call(se_own_kernel, shapes, se_scratch(own), 25 << 20, 2 << 20)(x, *rest)


def se_halo_call(x, *rest):
    own, width = x.shape
    rows = HALO + CHUNK
    shapes = (jax.ShapeDtypeStruct((rows, width), jnp.bfloat16), jax.ShapeDtypeStruct((2, own), jnp.float32))
    return call(se_halo_kernel, shapes, se_scratch(rows), 25 << 20, 2 << 20)(x, *rest)


def mr_call(early, mid, *rest):
    own, width = mid.shape
    ext = HALO + own
    scratch = [
        pltpu.VMEM((ext, LANES), jnp.float32),
        pltpu.VMEM((FEAT_TAPS - 1, ext, LANES), jnp.float32),
        pltpu.VMEM((PAD + ext, LANES), jnp.float32),
        pltpu.VMEM((own + LANES, LANES), jnp.bfloat16),
        pltpu.VMEM((own, LANES), jnp.float32),
        pltpu.VMEM((own // LANES, LANES, 2 * LANES), jnp.bfloat16),
        pltpu.VMEM((own // LANES, (LANES // GROUP) * LANES, 2 * LANES), jnp.bfloat16),
    ]
    return call(mr_kernel, jax.ShapeDtypeStruct((own, width), jnp.bfloat16), scratch, 1 << 30, 4 << 20)(early, mid, *rest)


def shards(hidden, doc_lengths, gain_se, gain_mr, feat_se, feat_mr, filter_se, filter_mr):
    f32 = jnp.float32
    shape = jax.ShapeDtypeStruct
    own, width = hidden.shape[1:]
    groups = filter_se.shape[0]
    x = hidden[0]
    first = (lax.axis_index("ctx") * own).astype(jnp.int32).reshape(1)
    halo = shifted(x[own - HALO :], "ctx", 1)
    part = call(sums_kernel, shape((1, own), f32), [], 1 << 20, 1 << 20)(x)
    total = jnp.sum(lax.all_gather(part, "tp"), axis=0)
    before = shifted(total, "ctx", 1)
    off, fexp = call(
        place_kernel, (shape((HALO + own, LANES), f32), shape((8, width), f32)), [], 1 << 24, 1 << 20, smem=1
    )(first, total, doc_lengths, filter_se)
    base = call(
        turn_kernel, shape((groups, GROUP, LANES), f32), [pltpu.VMEM((groups, LANES), f32)], 1 << 24, 1 << 20
    )(total, filter_mr)
    gain = gain_se.reshape(1, width)
    mid, part_two = se_own_call(x, total, off, gain, feat_se, fexp)
    early, part_two = se_halo_call(x, halo, total, before, part_two, off, gain, feat_se, fexp)
    sums_two = lax.all_gather(part_two, "tp")
    return mr_call(early, mid, sums_two, off, gain_mr.reshape(1, width), feat_mr, base)[None]


def solution(mesh):
    in_specs = (
        P(None, "ctx", "tp"),
        P(),
        P("tp"),
        P("tp"),
        P(None, None, "tp"),
        P(None, None, "tp"),
        P("tp", None),
        P("tp", None),
    )
    out_specs = P(None, "ctx", "tp")
    return jax.shard_map(shards, mesh=mesh, in_specs=in_specs, out_specs=out_specs, check_vma=False)
```

```python
import jax
import jax.numpy as jnp
from jax import lax
from jax.experimental import pallas as pl
from jax.experimental.pallas import tpu as pltpu
from jax.sharding import PartitionSpec as P

D = 8192
FEAT_TAPS = 3
SHORT_TAPS = 7
MEDIUM_TAPS = 128
HALO = 144
LANES = 128
GROUP = 16
CHUNK = 16
PAD = 8

norm_epsilon = 1e-06
VMEM_LIMIT = 48 * 1024 * 1024


def shifted(x, axis, by):
    peers = lax.axis_size(axis)
    pairs = [(i, i + by) for i in range(peers) if 0 <= i + by < peers]
    return lax.ppermute(x, axis, pairs)


def turned(x, axis, by):
    peers = lax.axis_size(axis)
    return lax.ppermute(x, axis, [(i, (i + by) % peers) for i in range(peers)])


def as_row(column):
    rows = column.shape[0]
    return jnp.broadcast_to(column, (rows, LANES)).T[0:1]


def as_column(row):
    return jnp.broadcast_to(row, (LANES, row.shape[1])).T


def sums_kernel(x_ref, s_ref):
    rows, width = x_ref.shape
    for r in range(0, rows, 64):
        total = jnp.zeros((64, LANES), jnp.float32)
        for c in range(0, width, LANES):
            x = x_ref[r : r + 64, c : c + LANES].astype(jnp.float32)
            total = total + x * x
        col = jnp.sum(total, axis=1, keepdims=True)
        if r % 128 == 0:
            held = col
        else:
            s_ref[0:1, r - 64 : r + 64] = as_row(jnp.concatenate([held, col], axis=0))


def place_kernel(first_ref, len_ref, fse_ref, off_ref, fexp_ref):
    ext = off_ref.shape[0]
    width = fexp_ref.shape[1]
    groups = fse_ref.shape[0]
    lens = jnp.broadcast_to(len_ref[0:1, :].astype(jnp.float32), (8, LANES))
    lane = lax.broadcasted_iota(jnp.int32, (8, LANES), 1)
    ends = lens
    step = 1
    while step < LANES:
        ends = ends + jnp.where(lane >= step, pltpu.roll(ends, step, 1), 0.0)
        step *= 2
    starts = (ends - lens)[0:1]
    first = first_ref[0] - HALO
    for r in range(0, ext, CHUNK):
        pos = (lax.broadcasted_iota(jnp.int32, (CHUNK, LANES), 0) + (first + r)).astype(jnp.float32)
        doc_first = jnp.max(jnp.where(starts <= pos, starts, 0.0), axis=1, keepdims=True)
        off_ref[r : r + CHUNK, :] = pos - doc_first
    fse = fse_ref[...]
    for c in range(0, width, LANES):
        row = lax.broadcasted_iota(jnp.int32, (groups, LANES), 0)
        col = lax.broadcasted_iota(jnp.int32, (groups, LANES), 1)
        spread = (row == (c + col) // GROUP).astype(jnp.float32)
        fexp_ref[0:SHORT_TAPS, c : c + LANES] = lax.dot_general(
            fse, spread, (((0,), (0,)), ((), ())),
            preferred_element_type=jnp.float32, precision=lax.Precision.HIGHEST,
        )


def turn_kernel(after_ref, fmr_ref, base_ref, rev_ref):
    groups = fmr_ref.shape[0]
    rev_ref[...] = fmr_ref[...].astype(jnp.float32)

    def one(g, carry):
        h = jnp.broadcast_to(rev_ref[pl.ds(g, 1), :], (GROUP, LANES))
        base_ref[g] = pltpu.roll(h, 0, 1, stride=1, stride_axis=0)
        return carry

    lax.fori_loop(0, groups, one, 0, unroll=8)


def scale_of(total):
    return lax.rsqrt(total / D + norm_epsilon)


def scale_columns(sums_ref, scale_ref):
    total = sums_ref[0][...]
    for other in sums_ref[1:]:
        total = total + other[...]
    scale = scale_of(total)
    own = scale.shape[1] // 2
    scale_ref[0:HALO, :] = as_column(scale[:, 0:own])[own - HALO :, :]
    scale_ref[HALO:, :] = as_column(scale[:, own:])


def masks_of(off_ref, mask_ref, taps, first=0):
    for r in range(0, mask_ref.shape[1], CHUNK):
        off = off_ref[first + r : first + r + CHUNK, :]
        for j in range(1, taps):
            mask_ref[j - 1, r : r + CHUNK, :] = (off >= j).astype(jnp.float32)


def se_rows(
    raw, rows, skip, width, gain_ref, feat_ref, fexp_ref, mid_ref,
    scale_ref, mask_ref, norm_ref, prod_ref, q_ref, acc_ref,
):
    norm_ref[0:PAD, :] = jnp.zeros((PAD, LANES), jnp.float32)
    prod_ref[0:PAD, :] = jnp.zeros((PAD, LANES), jnp.float32)
    acc_ref[...] = jnp.zeros(acc_ref.shape, jnp.float32)

    def tile(i, carry):
        cols = pl.ds(pl.multiple_of(i * LANES, LANES), LANES)
        gain = gain_ref[0:1, cols]
        for e in range(0, rows, CHUNK):
            n = raw(e, cols) * scale_ref[e : e + CHUNK, :] * gain
            norm_ref[PAD + e : PAD + e + CHUNK, :] = n.astype(jnp.bfloat16).astype(jnp.float32)
        taps = [[feat_ref[s, j : j + 1, cols] for j in range(FEAT_TAPS)] for s in range(3)]
        for e in range(0, rows, CHUNK):
            xs = [norm_ref[PAD + e : PAD + e + CHUNK, :]]
            for j in range(1, FEAT_TAPS):
                xs.append(norm_ref[PAD + e - j : PAD + e - j + CHUNK, :] * mask_ref[j - 1, e : e + CHUNK, :])
            q, k, v = (
                taps[s][0] * xs[0] + taps[s][1] * xs[1] + taps[s][2] * xs[2] for s in range(3)
            )
            prod_ref[PAD + e : PAD + e + CHUNK, :] = k * v
            q_ref[e : e + CHUNK, :] = q
        filt = [fexp_ref[j : j + 1, cols] for j in range(SHORT_TAPS)]
        for e in range(skip, rows, CHUNK):
            total = filt[0] * prod_ref[PAD + e : PAD + e + CHUNK, :]
            for j in range(1, SHORT_TAPS):
                total = total + filt[j] * (
                    prod_ref[PAD + e - j : PAD + e - j + CHUNK, :] * mask_ref[j - 1, e : e + CHUNK, :]
                )
            mid = (raw(e, cols) + q_ref[e : e + CHUNK, :] * total).astype(jnp.bfloat16)
            mid_ref[e : e + CHUNK, cols] = mid
            mid = mid.astype(jnp.float32)
            acc_ref[e : e + CHUNK, :] = acc_ref[e : e + CHUNK, :] + mid * mid
        return carry

    lax.fori_loop(0, width // LANES, tile, 0)


def se_own_kernel(
    x_ref, total_ref, off_ref, gain_ref, feat_ref, fexp_ref, mid_ref, s_ref, scale_ref, mask_ref, *scratch,
):
    own, width = x_ref.shape
    acc_ref = scratch[-1]
    scale_ref[...] = as_column(scale_of(total_ref[...]))
    masks_of(off_ref, mask_ref, SHORT_TAPS, HALO)
    mid_ref[0:CHUNK, :] = jnp.zeros((CHUNK, width), jnp.bfloat16)
    se_rows(
        lambda e, cols: x_ref[e : e + CHUNK, cols].astype(jnp.float32),
        own, CHUNK, width, gain_ref, feat_ref, fexp_ref, mid_ref, scale_ref, mask_ref, *scratch,
    )
    for r in range(0, own, LANES):
        s_ref[0:1, r : r + LANES] = as_row(jnp.sum(acc_ref[r : r + LANES, :], axis=1, keepdims=True))


def se_halo_kernel(
    x_ref, halo_ref, total_ref, before_ref, part_ref, off_ref, gain_ref, feat_ref, fexp_ref, mid_ref, s_ref,
    scale_ref, mask_ref, *scratch,
):
    own, width = x_ref.shape
    acc_ref = scratch[-1]
    scale_ref[0:HALO, :] = as_column(scale_of(before_ref[...]))[own - HALO :, :]
    scale_ref[HALO:, :] = as_column(scale_of(total_ref[...]))[0:CHUNK, :]
    masks_of(off_ref, mask_ref, SHORT_TAPS)

    def raw(e, cols):
        if e < HALO:
            return halo_ref[e : e + CHUNK, cols].astype(jnp.float32)
        return x_ref[e - HALO : e - HALO + CHUNK, cols].astype(jnp.float32)

    se_rows(
        raw, HALO + CHUNK, 0, width, gain_ref, feat_ref, fexp_ref, mid_ref, scale_ref, mask_ref, *scratch
    )
    halo_part = jnp.sum(acc_ref[0:HALO, :], axis=1, keepdims=True)
    halo_part = jnp.concatenate([jnp.zeros((own - HALO, 1), jnp.float32), halo_part], axis=0)
    own_part = jnp.sum(acc_ref[HALO:, :], axis=1, keepdims=True)
    own_part = jnp.concatenate([own_part, jnp.zeros((own - CHUNK, 1), jnp.float32)], axis=0)
    s_ref[0:1, 0:own] = as_row(halo_part)
    s_ref[0:1, own:] = as_row(own_part) + part_ref[...]


def mr_kernel(
    early_ref, mid_ref, sums0_ref, sums1_ref, sums2_ref, sums3_ref, off_ref, gain_ref, feat_ref, base_ref, out_ref,
    scale_ref, mask_ref, norm_ref, keep_ref, *slots,
):
    own, width = mid_ref.shape
    ext = HALO + own
    blocks = own // LANES
    per_tile = LANES // GROUP
    scale_columns((sums0_ref, sums1_ref, sums2_ref, sums3_ref), scale_ref)
    masks_of(off_ref, mask_ref, FEAT_TAPS)
    norm_ref[0:PAD, :] = jnp.zeros((PAD, LANES), jnp.float32)
    row = lax.broadcasted_iota(jnp.int32, (LANES, LANES), 0)
    col = lax.broadcasted_iota(jnp.int32, (LANES, LANES), 1)
    for b in range(blocks):
        off = off_ref[HALO + b * LANES : HALO + (b + 1) * LANES, :].T
        lag = (col - row).astype(jnp.float32)
        before = (row > col) & (lag + MEDIUM_TAPS <= off)
        within = (row <= col) & (lag <= off)
        at = slice(b * LANES, (b + 1) * LANES)
        keep_ref[0:LANES, at] = before.astype(jnp.float32).astype(jnp.bfloat16)
        keep_ref[LANES:, at] = within.astype(jnp.float32).astype(jnp.bfloat16)
    early = early_ref.shape[0]

    def middle(e, cols):
        held = early_ref[e : e + CHUNK, cols] if e < early else mid_ref[e - HALO : e - HALO + CHUNK, cols]
        return held.astype(jnp.float32)


    def ready(i, slot):
        mixed_ref, q_ref = slot
        cols = pl.ds(pl.multiple_of(i * LANES, LANES), LANES)
        gain = gain_ref[0:1, cols]
        for e in range(0, ext, CHUNK):
            n = middle(e, cols) * scale_ref[e : e + CHUNK, :] * gain
            norm_ref[PAD + e : PAD + e + CHUNK, :] = n.astype(jnp.bfloat16).astype(jnp.float32)
        taps = [[feat_ref[s, j : j + 1, cols] for j in range(FEAT_TAPS)] for s in range(3)]
        prods = []
        for e in range(HALO - LANES, ext, CHUNK):
            xs = [norm_ref[PAD + e : PAD + e + CHUNK, :]]
            for j in range(1, FEAT_TAPS):
                xs.append(norm_ref[PAD + e - j : PAD + e - j + CHUNK, :] * mask_ref[j - 1, e : e + CHUNK, :])
            k, v = (taps[s][0] * xs[0] + taps[s][1] * xs[1] + taps[s][2] * xs[2] for s in (1, 2))
            prods.append(k * v)
            if len(prods) == LANES // CHUNK:
                w = e + CHUNK - HALO
                mixed_ref[:, w : w + LANES] = jnp.concatenate(prods, axis=0).T.astype(jnp.bfloat16)
                prods = []
            if e >= HALO:
                q = taps[0][0] * xs[0] + taps[0][1] * xs[1] + taps[0][2] * xs[2]
                q_ref[e - HALO : e - HALO + CHUNK, :] = q

    def finish(i, slot):
        mixed_ref, q_ref = slot
        cols = pl.ds(pl.multiple_of(i * LANES, LANES), LANES)
        parts = [[] for _ in range(blocks)]
        for g in range(per_tile):
            base = base_ref[i * per_tile + g].astype(jnp.bfloat16)
            circ = jnp.concatenate([pltpu.roll(base, r, 1) if r else base for r in range(0, LANES, GROUP)], axis=0)
            rows = slice(g * GROUP, (g + 1) * GROUP)
            toep = jnp.concatenate([jnp.concatenate([circ] * blocks, axis=1)] * 2, axis=0) * keep_ref[...]
            window = jnp.concatenate(
                [mixed_ref[rows, b * LANES : (b + 2) * LANES] for b in range(blocks)], axis=0
            )
            y = jnp.dot(window, toep, preferred_element_type=jnp.float32)
            for b in range(blocks):
                parts[b].append(y[b * GROUP : (b + 1) * GROUP, b * LANES : (b + 1) * LANES])
        medium = [jnp.concatenate(part, axis=0).T for part in parts]
        for b in range(blocks):
            for r in range(0, LANES, CHUNK):
                t = b * LANES + r
                out = middle(HALO + t, cols) + q_ref[t : t + CHUNK, :] * medium[b][r : r + CHUNK]
                out_ref[t : t + CHUNK, cols] = out.astype(jnp.bfloat16)

    tiles = width // LANES
    slots = (slots[:2], slots[2:])
    ready(0, slots[0])

    def pair(j, carry):
        for at in range(2):
            i = 2 * j + at
            ready(jnp.minimum(i + 1, tiles - 1), slots[1 - at])
            finish(i, slots[at])
        return carry

    lax.fori_loop(0, tiles // 2, pair, 0)


def call(kernel, out_shape, scratch, flops, nbytes, smem=0):
    count = smem
    params = pltpu.CompilerParams(vmem_limit_bytes=VMEM_LIMIT)
    cost = pl.CostEstimate(flops=flops, bytes_accessed=nbytes, transcendentals=0)

    def run(*operands):
        specs = [pl.BlockSpec(memory_space=pltpu.SMEM)] * count
        specs += [pl.BlockSpec(memory_space=pltpu.VMEM)] * (len(operands) - count)
        return pl.pallas_call(
            kernel, out_shape=out_shape, in_specs=specs,
            out_specs=jax.tree.map(lambda _: pl.BlockSpec(memory_space=pltpu.VMEM), out_shape),
            scratch_shapes=scratch, compiler_params=params, cost_estimate=cost,
        )(*operands)

    return run


def se_scratch(rows):
    return [
        pltpu.VMEM((rows, LANES), jnp.float32),
        pltpu.VMEM((SHORT_TAPS - 1, rows, LANES), jnp.float32),
        pltpu.VMEM((PAD + rows, LANES), jnp.float32),
        pltpu.VMEM((PAD + rows, LANES), jnp.float32),
        pltpu.VMEM((rows, LANES), jnp.float32),
        pltpu.VMEM((rows, LANES), jnp.float32),
    ]


def se_own_call(x, *rest):
    own, width = x.shape
    shapes = (jax.ShapeDtypeStruct((own, width), jnp.bfloat16), jax.ShapeDtypeStruct((1, own), jnp.float32))
    return call(se_own_kernel, shapes, se_scratch(own), 25 << 20, 2 << 20)(x, *rest)


def se_halo_call(x, *rest):
    own, width = x.shape
    rows = HALO + CHUNK
    shapes = (jax.ShapeDtypeStruct((rows, width), jnp.bfloat16), jax.ShapeDtypeStruct((1, 2 * own), jnp.float32))
    return call(se_halo_kernel, shapes, se_scratch(rows), 25 << 20, 2 << 20)(x, *rest)


def mr_call(early, mid, *rest):
    own, width = mid.shape
    ext = HALO + own
    blocks = own // LANES
    slot = [
        pltpu.VMEM((LANES, own + LANES), jnp.bfloat16),
        pltpu.VMEM((own, LANES), jnp.float32),
    ]
    scratch = [
        pltpu.VMEM((ext, LANES), jnp.float32),
        pltpu.VMEM((FEAT_TAPS - 1, ext, LANES), jnp.float32),
        pltpu.VMEM((PAD + ext, LANES), jnp.float32),
        pltpu.VMEM((2 * LANES, blocks * LANES), jnp.bfloat16),
        *slot,
        *slot,
    ]
    return call(mr_kernel, jax.ShapeDtypeStruct((own, width), jnp.bfloat16), scratch, 1 << 30, 4 << 20)(early, mid, *rest)


def shards(hidden, doc_lengths, gain_se, gain_mr, feat_se, feat_mr, filter_se, filter_mr):
    f32 = jnp.float32
    shape = jax.ShapeDtypeStruct
    own, width = hidden.shape[1:]
    groups = filter_se.shape[0]
    x = hidden[0]
    first = (lax.axis_index("ctx") * own).astype(jnp.int32).reshape(1)
    halo = shifted(x[own - HALO :], "ctx", 1)
    part = call(sums_kernel, shape((1, own), f32), [], 1 << 20, 1 << 20)(x)
    total = part + turned(part, "tp", 3) + turned(part, "tp", 1) + turned(part, "tp", 2)
    before = shifted(total, "ctx", 1)
    off, fexp = call(
        place_kernel, (shape((HALO + own, LANES), f32), shape((8, width), f32)), [], 1 << 24, 1 << 20, smem=1
    )(first, doc_lengths, filter_se)
    base = call(
        turn_kernel, shape((groups, GROUP, LANES), f32), [pltpu.VMEM((groups, LANES), f32)], 1 << 24, 1 << 20
    )(total, filter_mr)
    gain = gain_se.reshape(1, width)
    mid, part_two = se_own_call(x, total, off, gain, feat_se, fexp)
    early, part_two = se_halo_call(x, halo, total, before, part_two, off, gain, feat_se, fexp)
    sums_two = [part_two] + [turned(part_two, "tp", by) for by in (3, 1, 2)]
    return mr_call(early, mid, *sums_two, off, gain_mr.reshape(1, width), feat_mr, base)[None]


def solution(mesh):
    in_specs = (
        P(None, "ctx", "tp"),
        P(),
        P("tp"),
        P("tp"),
        P(None, None, "tp"),
        P(None, None, "tp"),
        P("tp", None),
        P("tp", None),
    )
    out_specs = P(None, "ctx", "tp")
    return jax.shard_map(shards, mesh=mesh, in_specs=in_specs, out_specs=out_specs, check_vma=False)
```

```python
import jax
import jax.numpy as jnp
from jax import lax
from jax.experimental import pallas as pl
from jax.experimental.pallas import tpu as pltpu
from jax.sharding import PartitionSpec as P

D = 8192
FEAT_TAPS = 3
SHORT_TAPS = 7
MEDIUM_TAPS = 128
HALO = 144
LANES = 128
GROUP = 16
CHUNK = 16
PAD = 8

norm_epsilon = 1e-06
VMEM_LIMIT = 48 * 1024 * 1024


def shifted(x, axis, by):
    peers = lax.axis_size(axis)
    pairs = [(i, i + by) for i in range(peers) if 0 <= i + by < peers]
    return lax.ppermute(x, axis, pairs)


def turned(x, axis, by):
    peers = lax.axis_size(axis)
    return lax.ppermute(x, axis, [(i, (i + by) % peers) for i in range(peers)])


def lane_sums(held):
    return jnp.sum(held.T, axis=0, keepdims=True)


def as_column(row):
    rows = row.shape[1]
    return jnp.broadcast_to(jnp.broadcast_to(row, (8, rows)).T[:, 0:1], (rows, LANES))


def sums_kernel(x_ref, s_ref):
    rows, width = x_ref.shape
    for r in range(0, rows, LANES):
        total = []
        for h in range(r, r + LANES, 32):
            part = jnp.zeros((32, LANES), jnp.float32)
            for c in range(0, width, LANES):
                x = x_ref[h : h + 32, c : c + LANES].astype(jnp.float32)
                part = part + x * x
            total.append(part)
        s_ref[0:1, r : r + LANES] = lane_sums(jnp.concatenate(total, axis=0))


def place_kernel(first_ref, len_ref, fse_ref, off_ref, fexp_ref):
    ext = off_ref.shape[0]
    width = fexp_ref.shape[1]
    groups = fse_ref.shape[0]
    lens = jnp.broadcast_to(len_ref[0:1, :].astype(jnp.float32), (8, LANES))
    lane = lax.broadcasted_iota(jnp.int32, (8, LANES), 1)
    ends = lens
    step = 1
    while step < LANES:
        ends = ends + jnp.where(lane >= step, pltpu.roll(ends, step, 1), 0.0)
        step *= 2
    starts = (ends - lens)[0:1]
    first = first_ref[0] - HALO
    for r in range(0, ext, CHUNK):
        pos = (lax.broadcasted_iota(jnp.int32, (CHUNK, LANES), 0) + (first + r)).astype(jnp.float32)
        doc_first = jnp.max(jnp.where(starts <= pos, starts, 0.0), axis=1, keepdims=True)
        off = jnp.broadcast_to(pos - doc_first, (CHUNK, LANES))
        off_ref[r : r + CHUNK, :] = off
    fse = fse_ref[...]
    for c in range(0, width, LANES):
        row = lax.broadcasted_iota(jnp.int32, (groups, LANES), 0)
        col = lax.broadcasted_iota(jnp.int32, (groups, LANES), 1)
        spread = (row == (c + col) // GROUP).astype(jnp.float32)
        fexp_ref[0:SHORT_TAPS, c : c + LANES] = lax.dot_general(
            fse, spread, (((0,), (0,)), ((), ())),
            preferred_element_type=jnp.float32, precision=lax.Precision.HIGHEST,
        )


def turn_kernel(after_ref, fmr_ref, off_ref, base_ref, keep_ref, rev_ref):
    groups = fmr_ref.shape[0]
    rev_ref[...] = fmr_ref[...].astype(jnp.float32)

    def one(g, carry):
        h = jnp.broadcast_to(rev_ref[pl.ds(g, 1), :], (GROUP, LANES))
        base_ref[g] = pltpu.roll(h, 0, 1, stride=1, stride_axis=0).astype(jnp.bfloat16)
        return carry

    lax.fori_loop(0, groups, one, 0, unroll=8)
    row = lax.broadcasted_iota(jnp.int32, (LANES, LANES), 0)
    col = lax.broadcasted_iota(jnp.int32, (LANES, LANES), 1)
    lag = (col - row).astype(jnp.float32)
    for b in range(keep_ref.shape[1] // LANES):
        off = off_ref[HALO + b * LANES : HALO + (b + 1) * LANES, :].T
        before = (row > col) & (lag + MEDIUM_TAPS <= off)
        within = (row <= col) & (lag <= off)
        at = slice(b * LANES, (b + 1) * LANES)
        keep_ref[0:LANES, at] = before.astype(jnp.float32).astype(jnp.bfloat16)
        keep_ref[LANES:, at] = within.astype(jnp.float32).astype(jnp.bfloat16)


def scale_of(total):
    return lax.rsqrt(total / D + norm_epsilon)


def scale_columns(sums_ref, scale_ref):
    total = sums_ref[0][...]
    for other in sums_ref[1:]:
        total = total + other[...]
    scale = scale_of(total)
    own = scale.shape[1] // 2
    scale_ref[0:HALO, :] = as_column(scale[:, 0:own])[own - HALO :, :]
    scale_ref[HALO:, :] = as_column(scale[:, own:])


def masks_of(off_ref, mask_ref, taps, first=0):
    for r in range(0, mask_ref.shape[1], CHUNK):
        off = off_ref[first + r : first + r + CHUNK, :]
        for j in range(1, taps):
            mask_ref[j - 1, r : r + CHUNK, :] = (off >= j).astype(jnp.float32)


def se_rows(
    raw, rows, skip, width, mask_ref, gain_ref, feat_ref, fexp_ref, mid_ref,
    scale_ref, norm_ref, prod_ref, q_ref, acc_ref,
):
    norm_ref[0:PAD, :] = jnp.zeros((PAD, LANES), jnp.float32)
    prod_ref[0:PAD, :] = jnp.zeros((PAD, LANES), jnp.float32)
    acc_ref[...] = jnp.zeros(acc_ref.shape, jnp.float32)

    def tile(i, carry):
        cols = pl.ds(pl.multiple_of(i * LANES, LANES), LANES)
        gain = gain_ref[0:1, cols]
        for e in range(0, rows, CHUNK):
            norm_ref[PAD + e : PAD + e + CHUNK, :] = raw(e, cols) * scale_ref[e : e + CHUNK, :]
        taps = [[feat_ref[s, j : j + 1, cols] * gain for j in range(FEAT_TAPS)] for s in range(3)]
        for e in range(0, rows, CHUNK):
            xs = [norm_ref[PAD + e : PAD + e + CHUNK, :]]
            for j in range(1, FEAT_TAPS):
                xs.append(norm_ref[PAD + e - j : PAD + e - j + CHUNK, :] * mask_ref[j - 1, e : e + CHUNK, :])
            q, k, v = (
                taps[s][0] * xs[0] + taps[s][1] * xs[1] + taps[s][2] * xs[2] for s in range(3)
            )
            prod_ref[PAD + e : PAD + e + CHUNK, :] = k * v
            q_ref[e : e + CHUNK, :] = q
        filt = [fexp_ref[j : j + 1, cols] for j in range(SHORT_TAPS)]
        for e in range(skip, rows, CHUNK):
            total = filt[0] * prod_ref[PAD + e : PAD + e + CHUNK, :]
            for j in range(1, SHORT_TAPS):
                total = total + filt[j] * (
                    prod_ref[PAD + e - j : PAD + e - j + CHUNK, :] * mask_ref[j - 1, e : e + CHUNK, :]
                )
            mid = raw(e, cols) + q_ref[e : e + CHUNK, :] * total
            mid_ref[e : e + CHUNK, cols] = mid.astype(jnp.bfloat16)
            acc_ref[e : e + CHUNK, :] = acc_ref[e : e + CHUNK, :] + mid * mid
        return carry

    lax.fori_loop(0, width // LANES, tile, 0, unroll=2)


def se_own_kernel(
    x_ref, total_ref, off_ref, gain_ref, feat_ref, fexp_ref, mid_ref, s_ref, scale_ref, mask_ref, *scratch,
):
    own, width = x_ref.shape
    acc_ref = scratch[-1]
    scale_ref[...] = as_column(scale_of(total_ref[...]))
    masks_of(off_ref, mask_ref, SHORT_TAPS, HALO)
    mid_ref[0:CHUNK, :] = jnp.zeros((CHUNK, width), jnp.bfloat16)
    se_rows(
        lambda e, cols: x_ref[e : e + CHUNK, cols].astype(jnp.float32),
        own, CHUNK, width, mask_ref, gain_ref, feat_ref, fexp_ref, mid_ref, scale_ref, *scratch,
    )
    for r in range(0, own, LANES):
        s_ref[0:1, r : r + LANES] = lane_sums(acc_ref[r : r + LANES, :])


def se_halo_kernel(
    x_ref, halo_ref, total_ref, before_ref, part_ref, off_ref, gain_ref, feat_ref, fexp_ref, mid_ref, s_ref,
    scale_ref, mask_ref, *scratch,
):
    own, width = x_ref.shape
    acc_ref = scratch[-1]
    edge = LANES - CHUNK
    scale_ref[0:HALO, :] = as_column(scale_of(before_ref[...]))[own - HALO :, :]
    scale_ref[HALO:, :] = as_column(scale_of(total_ref[:, 0:LANES]))[0:CHUNK, :]
    masks_of(off_ref, mask_ref, SHORT_TAPS)

    def raw(e, cols):
        if e < HALO:
            return halo_ref[e : e + CHUNK, cols].astype(jnp.float32)
        return x_ref[e - HALO : e - HALO + CHUNK, cols].astype(jnp.float32)

    se_rows(
        raw, HALO + CHUNK, 0, width, mask_ref, gain_ref, feat_ref, fexp_ref, mid_ref, scale_ref, *scratch
    )
    pad = jnp.zeros((edge, LANES), jnp.float32)
    s_ref[0:1, 0:LANES] = lane_sums(jnp.concatenate([pad, acc_ref[0:CHUNK, :]], axis=0))
    s_ref[0:1, LANES:own] = lane_sums(acc_ref[CHUNK:HALO, :])
    s_ref[0:1, own : own + LANES] = part_ref[:, 0:LANES] + lane_sums(
        jnp.concatenate([acc_ref[HALO:, :], pad], axis=0)
    )
    s_ref[0:1, own + LANES :] = part_ref[:, LANES:]


def mr_kernel(
    early_ref, mid_ref, sums0_ref, sums1_ref, sums2_ref, sums3_ref, off_ref, gain_ref, feat_ref,
    base_ref, keep_ref, result_ref, out_ref, sems, scale_ref, mask_ref, norm_ref, *slots,
):
    own, width = mid_ref.shape
    ext = HALO + own
    blocks = own // LANES
    per_tile = LANES // GROUP
    scale_columns((sums0_ref, sums1_ref, sums2_ref, sums3_ref), scale_ref)
    masks_of(off_ref, mask_ref, FEAT_TAPS)
    norm_ref[0:PAD, :] = jnp.zeros((PAD, LANES), jnp.float32)
    early = early_ref.shape[0]

    def middle(e, cols):
        held = early_ref[e : e + CHUNK, cols] if e < early else mid_ref[e - HALO : e - HALO + CHUNK, cols]
        return held.astype(jnp.float32)


    def ready(i, slot):
        mixed_ref, q_ref = slot
        cols = pl.ds(pl.multiple_of(i * LANES, LANES), LANES)
        gain = gain_ref[0:1, cols]
        for e in range(0, ext, CHUNK):
            norm_ref[PAD + e : PAD + e + CHUNK, :] = middle(e, cols) * scale_ref[e : e + CHUNK, :]
        taps = [[feat_ref[s, j : j + 1, cols] * gain for j in range(FEAT_TAPS)] for s in range(3)]
        prods = []
        for e in range(HALO - LANES, ext, CHUNK):
            xs = [norm_ref[PAD + e : PAD + e + CHUNK, :]]
            for j in range(1, FEAT_TAPS):
                xs.append(norm_ref[PAD + e - j : PAD + e - j + CHUNK, :] * mask_ref[j - 1, e : e + CHUNK, :])
            k, v = (taps[s][0] * xs[0] + taps[s][1] * xs[1] + taps[s][2] * xs[2] for s in (1, 2))
            prods.append(k * v)
            if len(prods) == LANES // CHUNK:
                w = e + CHUNK - HALO
                mixed_ref[:, w : w + LANES] = jnp.concatenate(prods, axis=0).T.astype(jnp.bfloat16)
                prods = []
            if e >= HALO:
                q = taps[0][0] * xs[0] + taps[0][1] * xs[1] + taps[0][2] * xs[2]
                q_ref[e - HALO : e - HALO + CHUNK, :] = q

    def finish(i, slot):
        mixed_ref, q_ref = slot
        cols = pl.ds(pl.multiple_of(i * LANES, LANES), LANES)
        parts = [[] for _ in range(blocks)]
        for g in range(per_tile):
            base = base_ref[i * per_tile + g]
            circ = jnp.concatenate([pltpu.roll(base, r, 1) if r else base for r in range(0, LANES, GROUP)], axis=0)
            rows = slice(g * GROUP, (g + 1) * GROUP)
            toep = jnp.concatenate([jnp.concatenate([circ] * blocks, axis=1)] * 2, axis=0) * keep_ref[...]
            window = jnp.concatenate(
                [mixed_ref[rows, b * LANES : (b + 2) * LANES] for b in range(blocks)], axis=0
            )
            y = jnp.dot(window, toep, preferred_element_type=jnp.float32)
            for b in range(blocks):
                parts[b].append(y[b * GROUP : (b + 1) * GROUP, b * LANES : (b + 1) * LANES])
        medium = [jnp.concatenate(part, axis=0).T for part in parts]
        for b in range(blocks):
            for r in range(0, LANES, CHUNK):
                t = b * LANES + r
                out = middle(HALO + t, cols) + q_ref[t : t + CHUNK, :] * medium[b][r : r + CHUNK]
                out_ref[t : t + CHUNK, cols] = out.astype(jnp.bfloat16)

    tiles = width // LANES
    slots = (slots[:2], slots[2:])
    ready(0, slots[0])

    def leave(j):
        cols = pl.ds(pl.multiple_of(j * 2 * LANES, 2 * LANES), 2 * LANES)
        return pltpu.make_async_copy(out_ref.at[:, cols], result_ref.at[:, cols], sems.at[j])

    def pair(j, carry):
        for at in range(2):
            i = 2 * j + at
            ready(jnp.minimum(i + 1, tiles - 1), slots[1 - at])
            finish(i, slots[at])
        leave(j).start()
        return carry

    lax.fori_loop(0, tiles // 2, pair, 0, unroll=4)
    for j in range(tiles // 2):
        leave(j).wait()


def call(kernel, out_shape, scratch, flops, nbytes, smem=0, space=pltpu.VMEM):
    count = smem
    params = pltpu.CompilerParams(vmem_limit_bytes=VMEM_LIMIT)
    cost = pl.CostEstimate(flops=flops, bytes_accessed=nbytes, transcendentals=0)

    def run(*operands):
        specs = [pl.BlockSpec(memory_space=pltpu.SMEM)] * count
        specs += [pl.BlockSpec(memory_space=pltpu.VMEM)] * (len(operands) - count)
        return pl.pallas_call(
            kernel, out_shape=out_shape, in_specs=specs,
            out_specs=jax.tree.map(lambda _: pl.BlockSpec(memory_space=space), out_shape),
            scratch_shapes=scratch, compiler_params=params, cost_estimate=cost,
        )(*operands)

    return run


def se_scratch(rows):
    return [
        pltpu.VMEM((rows, LANES), jnp.float32),
        pltpu.VMEM((SHORT_TAPS - 1, rows, LANES), jnp.float32),
        pltpu.VMEM((PAD + rows, LANES), jnp.float32),
        pltpu.VMEM((PAD + rows, LANES), jnp.float32),
        pltpu.VMEM((rows, LANES), jnp.float32),
        pltpu.VMEM((rows, LANES), jnp.float32),
    ]


def se_own_call(x, *rest):
    own, width = x.shape
    shapes = (jax.ShapeDtypeStruct((own, width), jnp.bfloat16), jax.ShapeDtypeStruct((1, own), jnp.float32))
    return call(se_own_kernel, shapes, se_scratch(own), 25 << 20, 2 << 20)(x, *rest)


def se_halo_call(x, *rest):
    own, width = x.shape
    rows = HALO + CHUNK
    shapes = (jax.ShapeDtypeStruct((rows, width), jnp.bfloat16), jax.ShapeDtypeStruct((1, 2 * own), jnp.float32))
    return call(se_halo_kernel, shapes, se_scratch(rows), 25 << 20, 2 << 20)(x, *rest)


def mr_call(early, mid, *rest):
    own, width = mid.shape
    ext = HALO + own
    blocks = own // LANES
    slot = [
        pltpu.VMEM((LANES, own + LANES), jnp.bfloat16),
        pltpu.VMEM((own, LANES), jnp.float32),
    ]
    scratch = [
        pltpu.VMEM((own, width), jnp.bfloat16),
        pltpu.SemaphoreType.DMA((width // (2 * LANES),)),
        pltpu.VMEM((ext, LANES), jnp.float32),
        pltpu.VMEM((FEAT_TAPS - 1, ext, LANES), jnp.float32),
        pltpu.VMEM((PAD + ext, LANES), jnp.float32),
        *slot,
        *slot,
    ]
    return call(mr_kernel, jax.ShapeDtypeStruct((own, width), jnp.bfloat16), scratch, 1 << 30, 4 << 20, space=pl.ANY)(early, mid, *rest)


def shards(hidden, doc_lengths, gain_se, gain_mr, feat_se, feat_mr, filter_se, filter_mr):
    f32 = jnp.float32
    shape = jax.ShapeDtypeStruct
    own, width = hidden.shape[1:]
    groups = filter_se.shape[0]
    x = hidden[0]
    first = (lax.axis_index("ctx") * own).astype(jnp.int32).reshape(1)
    halo = shifted(x[own - HALO :], "ctx", 1)
    part = call(sums_kernel, shape((1, own), f32), [], 1 << 20, 1 << 20)(x)
    total = part + turned(part, "tp", 3) + turned(part, "tp", 1) + turned(part, "tp", 2)
    before = shifted(total, "ctx", 1)
    ext = HALO + own
    off, fexp = call(
        place_kernel,
        (shape((ext, LANES), f32), shape((8, width), f32)),
        [], 1 << 24, 1 << 20, smem=1,
    )(first, doc_lengths, filter_se)
    base, keep = call(
        turn_kernel,
        (shape((groups, GROUP, LANES), jnp.bfloat16), shape((2 * LANES, own), jnp.bfloat16)),
        [pltpu.VMEM((groups, LANES), f32)], 1 << 24, 1 << 20,
    )(total, filter_mr, off)
    gain = gain_se.reshape(1, width)
    mid, part_two = se_own_call(x, total, off, gain, feat_se, fexp)
    early, part_two = se_halo_call(x, halo, total, before, part_two, off, gain, feat_se, fexp)
    sums_two = [part_two] + [turned(part_two, "tp", by) for by in (3, 1, 2)]
    return mr_call(early, mid, *sums_two, off, gain_mr.reshape(1, width), feat_mr, base, keep)[None]


def solution(mesh):
    in_specs = (
        P(None, "ctx", "tp"),
        P(),
        P("tp"),
        P("tp"),
        P(None, None, "tp"),
        P(None, None, "tp"),
        P("tp", None),
        P("tp", None),
    )
    out_specs = P(None, "ctx", "tp")
    return jax.shard_map(shards, mesh=mesh, in_specs=in_specs, out_specs=out_specs, check_vma=False)
```

```python
import jax
import jax.numpy as jnp
from jax import lax
from jax.experimental import pallas as pl
from jax.experimental.pallas import tpu as pltpu
from jax.sharding import PartitionSpec as P

D = 8192
FEAT_TAPS = 3
SHORT_TAPS = 7
MEDIUM_TAPS = 128
HALO = 144
LANES = 128
GROUP = 16
CHUNK = 16
PAD = 8

norm_epsilon = 1e-06
VMEM_LIMIT = 48 * 1024 * 1024


def shifted(x, axis, by):
    peers = lax.axis_size(axis)
    pairs = [(i, i + by) for i in range(peers) if 0 <= i + by < peers]
    return lax.ppermute(x, axis, pairs)


def turned(x, axis, by):
    peers = lax.axis_size(axis)
    return lax.ppermute(x, axis, [(i, (i + by) % peers) for i in range(peers)])


def lane_sums(held):
    return jnp.sum(held.T, axis=0, keepdims=True)


def as_column(row):
    rows = row.shape[1]
    return jnp.broadcast_to(jnp.broadcast_to(row, (8, rows)).T[:, 0:1], (rows, LANES))


def sums_kernel(x_ref, s_ref):
    rows, width = x_ref.shape
    for r in range(0, rows, LANES):
        total = []
        for h in range(r, r + LANES, 32):
            part = jnp.zeros((32, LANES), jnp.float32)
            for c in range(0, width, LANES):
                x = x_ref[h : h + 32, c : c + LANES].astype(jnp.float32)
                part = part + x * x
            total.append(part)
        s_ref[0:1, r : r + LANES] = lane_sums(jnp.concatenate(total, axis=0))


def place_kernel(first_ref, len_ref, fse_ref, off_ref, fexp_ref):
    ext = off_ref.shape[0]
    width = fexp_ref.shape[1]
    groups = fse_ref.shape[0]
    lens = jnp.broadcast_to(len_ref[0:1, :].astype(jnp.float32), (8, LANES))
    lane = lax.broadcasted_iota(jnp.int32, (8, LANES), 1)
    ends = lens
    step = 1
    while step < LANES:
        ends = ends + jnp.where(lane >= step, pltpu.roll(ends, step, 1), 0.0)
        step *= 2
    starts = (ends - lens)[0:1]
    first = first_ref[0] - HALO
    for r in range(0, ext, CHUNK):
        pos = (lax.broadcasted_iota(jnp.int32, (CHUNK, LANES), 0) + (first + r)).astype(jnp.float32)
        doc_first = jnp.max(jnp.where(starts <= pos, starts, 0.0), axis=1, keepdims=True)
        off = jnp.broadcast_to(pos - doc_first, (CHUNK, LANES))
        off_ref[r : r + CHUNK, :] = off
    fse = fse_ref[...]
    for c in range(0, width, LANES):
        row = lax.broadcasted_iota(jnp.int32, (groups, LANES), 0)
        col = lax.broadcasted_iota(jnp.int32, (groups, LANES), 1)
        spread = (row == (c + col) // GROUP).astype(jnp.float32)
        fexp_ref[0:SHORT_TAPS, c : c + LANES] = lax.dot_general(
            fse, spread, (((0,), (0,)), ((), ())),
            preferred_element_type=jnp.float32, precision=lax.Precision.HIGHEST,
        )


def turn_kernel(after_ref, fmr_ref, off_ref, base_ref, keep_ref, rev_ref):
    groups = fmr_ref.shape[0]
    rev_ref[...] = fmr_ref[...].astype(jnp.float32)

    def one(g, carry):
        h = jnp.broadcast_to(rev_ref[pl.ds(g, 1), :], (GROUP, LANES))
        base_ref[g] = pltpu.roll(h, 0, 1, stride=1, stride_axis=0).astype(jnp.bfloat16)
        return carry

    lax.fori_loop(0, groups, one, 0, unroll=8)
    row = lax.broadcasted_iota(jnp.int32, (LANES, LANES), 0)
    col = lax.broadcasted_iota(jnp.int32, (LANES, LANES), 1)
    lag = (col - row).astype(jnp.float32)
    for b in range(keep_ref.shape[1] // LANES):
        off = off_ref[HALO + b * LANES : HALO + (b + 1) * LANES, :].T
        before = (row > col) & (lag + MEDIUM_TAPS <= off)
        within = (row <= col) & (lag <= off)
        at = slice(b * LANES, (b + 1) * LANES)
        keep_ref[0:LANES, at] = before.astype(jnp.float32).astype(jnp.bfloat16)
        keep_ref[LANES:, at] = within.astype(jnp.float32).astype(jnp.bfloat16)


def scale_of(total):
    return lax.rsqrt(total / D + norm_epsilon)


def scale_columns(sums_ref, scale_ref):
    total = sums_ref[0][...]
    for other in sums_ref[1:]:
        total = total + other[...]
    scale = scale_of(total)
    own = scale.shape[1] // 2
    scale_ref[0:HALO, :] = as_column(scale[:, 0:own])[own - HALO :, :]
    scale_ref[HALO:, :] = as_column(scale[:, own:])


def masks_of(off_ref, mask_ref, taps, first=0):
    for r in range(0, mask_ref.shape[1], CHUNK):
        off = off_ref[first + r : first + r + CHUNK, :]
        for j in range(1, taps):
            mask_ref[j - 1, r : r + CHUNK, :] = (off >= j).astype(jnp.float32)


def se_rows(
    raw, rows, skip, width, mask_ref, gain_ref, feat_ref, fexp_ref, mid_ref,
    scale_ref, norm_ref, prod_ref, q_ref, acc_ref,
):
    norm_ref[0:PAD, :] = jnp.zeros((PAD, LANES), jnp.float32)
    prod_ref[0:PAD, :] = jnp.zeros((PAD, LANES), jnp.float32)
    acc_ref[...] = jnp.zeros(acc_ref.shape, jnp.float32)

    def tile(i, carry):
        cols = pl.ds(pl.multiple_of(i * LANES, LANES), LANES)
        gain = gain_ref[0:1, cols]
        for e in range(0, rows, CHUNK):
            n = (raw(e, cols) * scale_ref[e : e + CHUNK, :] * gain).astype(jnp.bfloat16)
            norm_ref[PAD + e : PAD + e + CHUNK, :] = n.astype(jnp.float32)
        taps = [[feat_ref[s, j : j + 1, cols] for j in range(FEAT_TAPS)] for s in range(3)]
        for e in range(0, rows, CHUNK):
            xs = [norm_ref[PAD + e : PAD + e + CHUNK, :]]
            for j in range(1, FEAT_TAPS):
                xs.append(norm_ref[PAD + e - j : PAD + e - j + CHUNK, :] * mask_ref[j - 1, e : e + CHUNK, :])
            q, k, v = (
                taps[s][0] * xs[0] + taps[s][1] * xs[1] + taps[s][2] * xs[2] for s in range(3)
            )
            prod_ref[PAD + e : PAD + e + CHUNK, :] = k * v
            q_ref[e : e + CHUNK, :] = q
        filt = [fexp_ref[j : j + 1, cols] for j in range(SHORT_TAPS)]
        for e in range(skip, rows, CHUNK):
            total = filt[0] * prod_ref[PAD + e : PAD + e + CHUNK, :]
            for j in range(1, SHORT_TAPS):
                total = total + filt[j] * (
                    prod_ref[PAD + e - j : PAD + e - j + CHUNK, :] * mask_ref[j - 1, e : e + CHUNK, :]
                )
            mid = raw(e, cols) + q_ref[e : e + CHUNK, :] * total
            mid_ref[e : e + CHUNK, cols] = mid.astype(jnp.bfloat16)
            acc_ref[e : e + CHUNK, :] = acc_ref[e : e + CHUNK, :] + mid * mid
        return carry

    lax.fori_loop(0, width // LANES, tile, 0, unroll=2)


def se_own_kernel(
    x_ref, total_ref, off_ref, gain_ref, feat_ref, fexp_ref, mid_ref, s_ref, scale_ref, mask_ref, *scratch,
):
    own, width = x_ref.shape
    acc_ref = scratch[-1]
    scale_ref[...] = as_column(scale_of(total_ref[...]))
    masks_of(off_ref, mask_ref, SHORT_TAPS, HALO)
    mid_ref[0:CHUNK, :] = jnp.zeros((CHUNK, width), jnp.bfloat16)
    se_rows(
        lambda e, cols: x_ref[e : e + CHUNK, cols].astype(jnp.float32),
        own, CHUNK, width, mask_ref, gain_ref, feat_ref, fexp_ref, mid_ref, scale_ref, *scratch,
    )
    for r in range(0, own, LANES):
        s_ref[0:1, r : r + LANES] = lane_sums(acc_ref[r : r + LANES, :])


def se_halo_kernel(
    x_ref, halo_ref, total_ref, before_ref, part_ref, off_ref, gain_ref, feat_ref, fexp_ref, mid_ref, s_ref,
    scale_ref, mask_ref, *scratch,
):
    own, width = x_ref.shape
    acc_ref = scratch[-1]
    edge = LANES - CHUNK
    scale_ref[0:HALO, :] = as_column(scale_of(before_ref[...]))[own - HALO :, :]
    scale_ref[HALO:, :] = as_column(scale_of(total_ref[:, 0:LANES]))[0:CHUNK, :]
    masks_of(off_ref, mask_ref, SHORT_TAPS)

    def raw(e, cols):
        if e < HALO:
            return halo_ref[e : e + CHUNK, cols].astype(jnp.float32)
        return x_ref[e - HALO : e - HALO + CHUNK, cols].astype(jnp.float32)

    se_rows(
        raw, HALO + CHUNK, 0, width, mask_ref, gain_ref, feat_ref, fexp_ref, mid_ref, scale_ref, *scratch
    )
    pad = jnp.zeros((edge, LANES), jnp.float32)
    s_ref[0:1, 0:LANES] = lane_sums(jnp.concatenate([pad, acc_ref[0:CHUNK, :]], axis=0))
    s_ref[0:1, LANES:own] = lane_sums(acc_ref[CHUNK:HALO, :])
    s_ref[0:1, own : own + LANES] = part_ref[:, 0:LANES] + lane_sums(
        jnp.concatenate([acc_ref[HALO:, :], pad], axis=0)
    )
    s_ref[0:1, own + LANES :] = part_ref[:, LANES:]


def mr_kernel(
    early_ref, mid_ref, sums0_ref, sums1_ref, sums2_ref, sums3_ref, off_ref, gain_ref, feat_ref,
    base_ref, keep_ref, result_ref, out_ref, sems, scale_ref, mask_ref, norm_ref, *slots,
):
    own, width = mid_ref.shape
    ext = HALO + own
    blocks = own // LANES
    per_tile = LANES // GROUP
    scale_columns((sums0_ref, sums1_ref, sums2_ref, sums3_ref), scale_ref)
    masks_of(off_ref, mask_ref, FEAT_TAPS)
    norm_ref[0:PAD, :] = jnp.zeros((PAD, LANES), jnp.float32)
    early = early_ref.shape[0]

    def middle(e, cols):
        held = early_ref[e : e + CHUNK, cols] if e < early else mid_ref[e - HALO : e - HALO + CHUNK, cols]
        return held.astype(jnp.float32)


    def ready(i, slot):
        mixed_ref, q_ref = slot
        cols = pl.ds(pl.multiple_of(i * LANES, LANES), LANES)
        gain = gain_ref[0:1, cols]
        for e in range(0, ext, CHUNK):
            n = (middle(e, cols) * scale_ref[e : e + CHUNK, :] * gain).astype(jnp.bfloat16)
            norm_ref[PAD + e : PAD + e + CHUNK, :] = n.astype(jnp.float32)
        taps = [[feat_ref[s, j : j + 1, cols] for j in range(FEAT_TAPS)] for s in range(3)]
        prods = []
        for e in range(HALO - LANES, ext, CHUNK):
            xs = [norm_ref[PAD + e : PAD + e + CHUNK, :]]
            for j in range(1, FEAT_TAPS):
                xs.append(norm_ref[PAD + e - j : PAD + e - j + CHUNK, :] * mask_ref[j - 1, e : e + CHUNK, :])
            k, v = (taps[s][0] * xs[0] + taps[s][1] * xs[1] + taps[s][2] * xs[2] for s in (1, 2))
            prods.append(k * v)
            if len(prods) == LANES // CHUNK:
                w = e + CHUNK - HALO
                mixed_ref[:, w : w + LANES] = jnp.concatenate(prods, axis=0).T.astype(jnp.bfloat16)
                prods = []
            if e >= HALO:
                q = taps[0][0] * xs[0] + taps[0][1] * xs[1] + taps[0][2] * xs[2]
                q_ref[e - HALO : e - HALO + CHUNK, :] = q

    def finish(i, slot):
        mixed_ref, q_ref = slot
        cols = pl.ds(pl.multiple_of(i * LANES, LANES), LANES)
        parts = [[] for _ in range(blocks)]
        for g in range(per_tile):
            base = base_ref[i * per_tile + g]
            circ = jnp.concatenate([pltpu.roll(base, r, 1) if r else base for r in range(0, LANES, GROUP)], axis=0)
            rows = slice(g * GROUP, (g + 1) * GROUP)
            toep = jnp.concatenate([jnp.concatenate([circ] * blocks, axis=1)] * 2, axis=0) * keep_ref[...]
            window = jnp.concatenate(
                [mixed_ref[rows, b * LANES : (b + 2) * LANES] for b in range(blocks)], axis=0
            )
            y = jnp.dot(window, toep, preferred_element_type=jnp.float32)
            for b in range(blocks):
                parts[b].append(y[b * GROUP : (b + 1) * GROUP, b * LANES : (b + 1) * LANES])
        medium = [jnp.concatenate(part, axis=0).T for part in parts]
        for b in range(blocks):
            for r in range(0, LANES, CHUNK):
                t = b * LANES + r
                out = middle(HALO + t, cols) + q_ref[t : t + CHUNK, :] * medium[b][r : r + CHUNK]
                out_ref[t : t + CHUNK, cols] = out.astype(jnp.bfloat16)

    tiles = width // LANES
    slots = (slots[:2], slots[2:])
    ready(0, slots[0])

    def leave(j):
        cols = pl.ds(pl.multiple_of(j * 2 * LANES, 2 * LANES), 2 * LANES)
        return pltpu.make_async_copy(out_ref.at[:, cols], result_ref.at[:, cols], sems.at[j])

    def pair(j, carry):
        for at in range(2):
            i = 2 * j + at
            ready(jnp.minimum(i + 1, tiles - 1), slots[1 - at])
            finish(i, slots[at])
        leave(j).start()
        return carry

    lax.fori_loop(0, tiles // 2, pair, 0, unroll=4)
    for j in range(tiles // 2):
        leave(j).wait()


def call(kernel, out_shape, scratch, flops, nbytes, smem=0, space=pltpu.VMEM):
    count = smem
    params = pltpu.CompilerParams(vmem_limit_bytes=VMEM_LIMIT)
    cost = pl.CostEstimate(flops=flops, bytes_accessed=nbytes, transcendentals=0)

    def run(*operands):
        specs = [pl.BlockSpec(memory_space=pltpu.SMEM)] * count
        specs += [pl.BlockSpec(memory_space=pltpu.VMEM)] * (len(operands) - count)
        return pl.pallas_call(
            kernel, out_shape=out_shape, in_specs=specs,
            out_specs=jax.tree.map(lambda _: pl.BlockSpec(memory_space=space), out_shape),
            scratch_shapes=scratch, compiler_params=params, cost_estimate=cost,
        )(*operands)

    return run


def se_scratch(rows):
    return [
        pltpu.VMEM((rows, LANES), jnp.float32),
        pltpu.VMEM((SHORT_TAPS - 1, rows, LANES), jnp.float32),
        pltpu.VMEM((PAD + rows, LANES), jnp.float32),
        pltpu.VMEM((PAD + rows, LANES), jnp.float32),
        pltpu.VMEM((rows, LANES), jnp.float32),
        pltpu.VMEM((rows, LANES), jnp.float32),
    ]


def se_own_call(x, *rest):
    own, width = x.shape
    shapes = (jax.ShapeDtypeStruct((own, width), jnp.bfloat16), jax.ShapeDtypeStruct((1, own), jnp.float32))
    return call(se_own_kernel, shapes, se_scratch(own), 25 << 20, 2 << 20)(x, *rest)


def se_halo_call(x, *rest):
    own, width = x.shape
    rows = HALO + CHUNK
    shapes = (jax.ShapeDtypeStruct((rows, width), jnp.bfloat16), jax.ShapeDtypeStruct((1, 2 * own), jnp.float32))
    return call(se_halo_kernel, shapes, se_scratch(rows), 25 << 20, 2 << 20)(x, *rest)


def mr_call(early, mid, *rest):
    own, width = mid.shape
    ext = HALO + own
    blocks = own // LANES
    slot = [
        pltpu.VMEM((LANES, own + LANES), jnp.bfloat16),
        pltpu.VMEM((own, LANES), jnp.float32),
    ]
    scratch = [
        pltpu.VMEM((own, width), jnp.bfloat16),
        pltpu.SemaphoreType.DMA((width // (2 * LANES),)),
        pltpu.VMEM((ext, LANES), jnp.float32),
        pltpu.VMEM((FEAT_TAPS - 1, ext, LANES), jnp.float32),
        pltpu.VMEM((PAD + ext, LANES), jnp.float32),
        *slot,
        *slot,
    ]
    return call(mr_kernel, jax.ShapeDtypeStruct((own, width), jnp.bfloat16), scratch, 1 << 30, 4 << 20, space=pl.ANY)(early, mid, *rest)


def shards(hidden, doc_lengths, gain_se, gain_mr, feat_se, feat_mr, filter_se, filter_mr):
    f32 = jnp.float32
    shape = jax.ShapeDtypeStruct
    own, width = hidden.shape[1:]
    groups = filter_se.shape[0]
    x = hidden[0]
    first = (lax.axis_index("ctx") * own).astype(jnp.int32).reshape(1)
    halo = shifted(x[own - HALO :], "ctx", 1)
    part = call(sums_kernel, shape((1, own), f32), [], 1 << 20, 1 << 20)(x)
    total = part + turned(part, "tp", 3) + turned(part, "tp", 2) + turned(part, "tp", 1)
    before = shifted(total, "ctx", 1)
    ext = HALO + own
    off, fexp = call(
        place_kernel,
        (shape((ext, LANES), f32), shape((8, width), f32)),
        [], 1 << 24, 1 << 20, smem=1,
    )(first, doc_lengths, filter_se)
    base, keep = call(
        turn_kernel,
        (shape((groups, GROUP, LANES), jnp.bfloat16), shape((2 * LANES, own), jnp.bfloat16)),
        [pltpu.VMEM((groups, LANES), f32)], 1 << 24, 1 << 20,
    )(total, filter_mr, off)
    gain = gain_se.reshape(1, width)
    mid, part_two = se_own_call(x, total, off, gain, feat_se, fexp)
    early, part_two = se_halo_call(x, halo, total, before, part_two, off, gain, feat_se, fexp)
    sums_two = [part_two] + [turned(part_two, "tp", by) for by in (3, 2, 1)]
    return mr_call(early, mid, *sums_two, off, gain_mr.reshape(1, width), feat_mr, base, keep)[None]


def solution(mesh):
    in_specs = (
        P(None, "ctx", "tp"),
        P(),
        P("tp"),
        P("tp"),
        P(None, None, "tp"),
        P(None, None, "tp"),
        P("tp", None),
        P("tp", None),
    )
    out_specs = P(None, "ctx", "tp")
    return jax.shard_map(shards, mesh=mesh, in_specs=in_specs, out_specs=out_specs, check_vma=False)
```

```python
import jax
import jax.numpy as jnp
from jax import lax
from jax.experimental import pallas as pl
from jax.experimental.pallas import tpu as pltpu
from jax.sharding import PartitionSpec as P

D = 8192
FEAT_TAPS = 3
SHORT_TAPS = 7
MEDIUM_TAPS = 128
HALO = 144
LANES = 128
GROUP = 16
CHUNK = 16
PAD = 8

norm_epsilon = 1e-06
VMEM_LIMIT = 48 * 1024 * 1024


def shifted(x, axis, by):
    peers = lax.axis_size(axis)
    pairs = [(i, i + by) for i in range(peers) if 0 <= i + by < peers]
    return lax.ppermute(x, axis, pairs)


def turned(x, axis, by):
    peers = lax.axis_size(axis)
    return lax.ppermute(x, axis, [(i, (i + by) % peers) for i in range(peers)])


def lane_sums(held):
    return jnp.sum(held.T, axis=0, keepdims=True)


def as_column(row):
    rows = row.shape[1]
    return jnp.broadcast_to(jnp.broadcast_to(row, (8, rows)).T[:, 0:1], (rows, LANES))


def sums_kernel(x_ref, s_ref):
    rows, width = x_ref.shape
    for r in range(0, rows, LANES):
        total = []
        for h in range(r, r + LANES, 32):
            part = jnp.zeros((32, LANES), jnp.float32)
            for c in range(0, width, LANES):
                x = x_ref[h : h + 32, c : c + LANES].astype(jnp.float32)
                part = part + x * x
            total.append(part)
        s_ref[0:1, r : r + LANES] = lane_sums(jnp.concatenate(total, axis=0))


def place_kernel(first_ref, len_ref, fse_ref, off_ref, fexp_ref):
    ext = off_ref.shape[0]
    width = fexp_ref.shape[1]
    groups = fse_ref.shape[0]
    lens = jnp.broadcast_to(len_ref[0:1, :].astype(jnp.float32), (8, LANES))
    lane = lax.broadcasted_iota(jnp.int32, (8, LANES), 1)
    ends = lens
    step = 1
    while step < LANES:
        ends = ends + jnp.where(lane >= step, pltpu.roll(ends, step, 1), 0.0)
        step *= 2
    starts = (ends - lens)[0:1]
    first = first_ref[0] - HALO
    for r in range(0, ext, CHUNK):
        pos = (lax.broadcasted_iota(jnp.int32, (CHUNK, LANES), 0) + (first + r)).astype(jnp.float32)
        doc_first = jnp.max(jnp.where(starts <= pos, starts, 0.0), axis=1, keepdims=True)
        off = jnp.broadcast_to(pos - doc_first, (CHUNK, LANES))
        off_ref[r : r + CHUNK, :] = off
    fse = fse_ref[...]
    for c in range(0, width, LANES):
        row = lax.broadcasted_iota(jnp.int32, (groups, LANES), 0)
        col = lax.broadcasted_iota(jnp.int32, (groups, LANES), 1)
        spread = (row == (c + col) // GROUP).astype(jnp.float32)
        fexp_ref[0:SHORT_TAPS, c : c + LANES] = lax.dot_general(
            fse, spread, (((0,), (0,)), ((), ())),
            preferred_element_type=jnp.float32, precision=lax.Precision.HIGHEST,
        )


def turn_kernel(after_ref, fmr_ref, off_ref, base_ref, keep_ref, rev_ref):
    groups = fmr_ref.shape[0]
    rev_ref[...] = fmr_ref[...].astype(jnp.float32)

    def one(g, carry):
        h = jnp.broadcast_to(rev_ref[pl.ds(g, 1), :], (GROUP, LANES))
        base_ref[g] = pltpu.roll(h, 0, 1, stride=1, stride_axis=0).astype(jnp.bfloat16)
        return carry

    lax.fori_loop(0, groups, one, 0, unroll=8)
    row = lax.broadcasted_iota(jnp.int32, (LANES, LANES), 0)
    col = lax.broadcasted_iota(jnp.int32, (LANES, LANES), 1)
    lag = (col - row).astype(jnp.float32)
    for b in range(keep_ref.shape[1] // LANES):
        off = off_ref[HALO + b * LANES : HALO + (b + 1) * LANES, :].T
        before = (row > col) & (lag + MEDIUM_TAPS <= off)
        within = (row <= col) & (lag <= off)
        at = slice(b * LANES, (b + 1) * LANES)
        keep_ref[0:LANES, at] = before.astype(jnp.float32).astype(jnp.bfloat16)
        keep_ref[LANES:, at] = within.astype(jnp.float32).astype(jnp.bfloat16)


def scale_of(total):
    return lax.rsqrt(total / D + norm_epsilon)


def scale_columns(sums_ref, scale_ref):
    total = sums_ref[0][...]
    for other in sums_ref[1:]:
        total = total + other[...]
    scale = scale_of(total)
    own = scale.shape[1] // 2
    scale_ref[0:HALO, :] = as_column(scale[:, 0:own])[own - HALO :, :]
    scale_ref[HALO:, :] = as_column(scale[:, own:])


def masks_of(off_ref, mask_ref, taps, first=0):
    for r in range(0, mask_ref.shape[1], CHUNK):
        off = off_ref[first + r : first + r + CHUNK, :]
        for j in range(1, taps):
            mask_ref[j - 1, r : r + CHUNK, :] = (off >= j).astype(jnp.float32)


def se_rows(
    raw, rows, skip, width, mask_ref, gain_ref, feat_ref, fexp_ref, mid_ref,
    scale_ref, norm_ref, prod_ref, q_ref, acc_ref,
):
    norm_ref[0:PAD, :] = jnp.zeros((PAD, LANES), jnp.float32)
    prod_ref[0:PAD, :] = jnp.zeros((PAD, LANES), jnp.float32)
    acc_ref[...] = jnp.zeros(acc_ref.shape, jnp.float32)

    def tile(i, carry):
        cols = pl.ds(pl.multiple_of(i * LANES, LANES), LANES)
        gain = gain_ref[0:1, cols]
        for e in range(0, rows, CHUNK):
            norm_ref[PAD + e : PAD + e + CHUNK, :] = raw(e, cols) * scale_ref[e : e + CHUNK, :]
        taps = [[feat_ref[s, j : j + 1, cols] * gain for j in range(FEAT_TAPS)] for s in range(3)]
        for e in range(0, rows, CHUNK):
            xs = [norm_ref[PAD + e : PAD + e + CHUNK, :]]
            for j in range(1, FEAT_TAPS):
                xs.append(norm_ref[PAD + e - j : PAD + e - j + CHUNK, :] * mask_ref[j - 1, e : e + CHUNK, :])
            q, k, v = (
                taps[s][0] * xs[0] + taps[s][1] * xs[1] + taps[s][2] * xs[2] for s in range(3)
            )
            prod_ref[PAD + e : PAD + e + CHUNK, :] = k * v
            q_ref[e : e + CHUNK, :] = q
        filt = [fexp_ref[j : j + 1, cols] for j in range(SHORT_TAPS)]
        for e in range(skip, rows, CHUNK):
            total = filt[0] * prod_ref[PAD + e : PAD + e + CHUNK, :]
            for j in range(1, SHORT_TAPS):
                total = total + filt[j] * (
                    prod_ref[PAD + e - j : PAD + e - j + CHUNK, :] * mask_ref[j - 1, e : e + CHUNK, :]
                )
            mid = raw(e, cols) + q_ref[e : e + CHUNK, :] * total
            mid_ref[e : e + CHUNK, cols] = mid.astype(jnp.bfloat16)
            acc_ref[e : e + CHUNK, :] = acc_ref[e : e + CHUNK, :] + mid * mid
        return carry

    lax.fori_loop(0, width // LANES, tile, 0, unroll=4)


def se_own_kernel(
    x_ref, total_ref, off_ref, gain_ref, feat_ref, fexp_ref, mid_ref, s_ref, scale_ref, mask_ref, *scratch,
):
    own, width = x_ref.shape
    acc_ref = scratch[-1]
    scale_ref[...] = as_column(scale_of(total_ref[...]))
    masks_of(off_ref, mask_ref, SHORT_TAPS, HALO)
    mid_ref[0:CHUNK, :] = jnp.zeros((CHUNK, width), jnp.bfloat16)
    se_rows(
        lambda e, cols: x_ref[e : e + CHUNK, cols].astype(jnp.float32),
        own, CHUNK, width, mask_ref, gain_ref, feat_ref, fexp_ref, mid_ref, scale_ref, *scratch,
    )
    for r in range(0, own, LANES):
        s_ref[0:1, r : r + LANES] = lane_sums(acc_ref[r : r + LANES, :])


def se_halo_kernel(
    x_ref, halo_ref, total_ref, before_ref, part_ref, off_ref, gain_ref, feat_ref, fexp_ref, mid_ref, s_ref,
    scale_ref, mask_ref, *scratch,
):
    own, width = x_ref.shape
    acc_ref = scratch[-1]
    edge = LANES - CHUNK
    scale_ref[0:HALO, :] = as_column(scale_of(before_ref[...]))[own - HALO :, :]
    scale_ref[HALO:, :] = as_column(scale_of(total_ref[:, 0:LANES]))[0:CHUNK, :]
    masks_of(off_ref, mask_ref, SHORT_TAPS)

    def raw(e, cols):
        if e < HALO:
            return halo_ref[e : e + CHUNK, cols].astype(jnp.float32)
        return x_ref[e - HALO : e - HALO + CHUNK, cols].astype(jnp.float32)

    se_rows(
        raw, HALO + CHUNK, 0, width, mask_ref, gain_ref, feat_ref, fexp_ref, mid_ref, scale_ref, *scratch
    )
    pad = jnp.zeros((edge, LANES), jnp.float32)
    s_ref[0:1, 0:LANES] = lane_sums(jnp.concatenate([pad, acc_ref[0:CHUNK, :]], axis=0))
    s_ref[0:1, LANES:own] = lane_sums(acc_ref[CHUNK:HALO, :])
    s_ref[0:1, own : own + LANES] = part_ref[:, 0:LANES] + lane_sums(
        jnp.concatenate([acc_ref[HALO:, :], pad], axis=0)
    )
    s_ref[0:1, own + LANES :] = part_ref[:, LANES:]


def mr_kernel(
    early_ref, mid_ref, sums0_ref, sums1_ref, sums2_ref, sums3_ref, off_ref, gain_ref, feat_ref,
    base_ref, keep_ref, result_ref, out_ref, sems, scale_ref, mask_ref, norm_ref, *slots,
):
    own, width = mid_ref.shape
    ext = HALO + own
    blocks = own // LANES
    per_tile = LANES // GROUP
    scale_columns((sums0_ref, sums1_ref, sums2_ref, sums3_ref), scale_ref)
    masks_of(off_ref, mask_ref, FEAT_TAPS)
    norm_ref[0:PAD, :] = jnp.zeros((PAD, LANES), jnp.float32)
    early = early_ref.shape[0]

    def middle(e, cols):
        held = early_ref[e : e + CHUNK, cols] if e < early else mid_ref[e - HALO : e - HALO + CHUNK, cols]
        return held.astype(jnp.float32)


    def ready(i, slot):
        mixed_ref, q_ref = slot
        cols = pl.ds(pl.multiple_of(i * LANES, LANES), LANES)
        gain = gain_ref[0:1, cols]
        for e in range(0, ext, CHUNK):
            norm_ref[PAD + e : PAD + e + CHUNK, :] = middle(e, cols) * scale_ref[e : e + CHUNK, :]
        taps = [[feat_ref[s, j : j + 1, cols] * gain for j in range(FEAT_TAPS)] for s in range(3)]
        prods = []
        for e in range(HALO - LANES, ext, CHUNK):
            xs = [norm_ref[PAD + e : PAD + e + CHUNK, :]]
            for j in range(1, FEAT_TAPS):
                xs.append(norm_ref[PAD + e - j : PAD + e - j + CHUNK, :] * mask_ref[j - 1, e : e + CHUNK, :])
            k, v = (taps[s][0] * xs[0] + taps[s][1] * xs[1] + taps[s][2] * xs[2] for s in (1, 2))
            prods.append(k * v)
            if len(prods) == LANES // CHUNK:
                w = e + CHUNK - HALO
                mixed_ref[:, w : w + LANES] = jnp.concatenate(prods, axis=0).T.astype(jnp.bfloat16)
                prods = []
            if e >= HALO:
                q = taps[0][0] * xs[0] + taps[0][1] * xs[1] + taps[0][2] * xs[2]
                q_ref[e - HALO : e - HALO + CHUNK, :] = q

    def finish(i, slot):
        mixed_ref, q_ref = slot
        cols = pl.ds(pl.multiple_of(i * LANES, LANES), LANES)
        parts = [[] for _ in range(blocks)]
        for g in range(per_tile):
            base = base_ref[i * per_tile + g]
            circ = jnp.concatenate([pltpu.roll(base, r, 1) if r else base for r in range(0, LANES, GROUP)], axis=0)
            rows = slice(g * GROUP, (g + 1) * GROUP)
            toep = jnp.concatenate([jnp.concatenate([circ] * blocks, axis=1)] * 2, axis=0) * keep_ref[...]
            window = jnp.concatenate(
                [mixed_ref[rows, b * LANES : (b + 2) * LANES] for b in range(blocks)], axis=0
            )
            y = jnp.dot(window, toep, preferred_element_type=jnp.float32)
            for b in range(blocks):
                parts[b].append(y[b * GROUP : (b + 1) * GROUP, b * LANES : (b + 1) * LANES])
        medium = [jnp.concatenate(part, axis=0).T for part in parts]
        for b in range(blocks):
            for r in range(0, LANES, CHUNK):
                t = b * LANES + r
                out = middle(HALO + t, cols) + q_ref[t : t + CHUNK, :] * medium[b][r : r + CHUNK]
                out_ref[t : t + CHUNK, cols] = out.astype(jnp.bfloat16)

    tiles = width // LANES
    slots = (slots[:2], slots[2:])
    ready(0, slots[0])

    def leave(j):
        cols = pl.ds(pl.multiple_of(j * 2 * LANES, 2 * LANES), 2 * LANES)
        return pltpu.make_async_copy(out_ref.at[:, cols], result_ref.at[:, cols], sems.at[j])

    for i in range(tiles):
        if i + 1 < tiles:
            ready(i + 1, slots[1 - i % 2])
        finish(i, slots[i % 2])
        if i % 2:
            leave(i // 2).start()
    for j in range(tiles // 2):
        leave(j).wait()


def call(kernel, out_shape, scratch, flops, nbytes, smem=0, space=pltpu.VMEM):
    count = smem
    params = pltpu.CompilerParams(vmem_limit_bytes=VMEM_LIMIT)
    cost = pl.CostEstimate(flops=flops, bytes_accessed=nbytes, transcendentals=0)

    def run(*operands):
        specs = [pl.BlockSpec(memory_space=pltpu.SMEM)] * count
        specs += [pl.BlockSpec(memory_space=pltpu.VMEM)] * (len(operands) - count)
        return pl.pallas_call(
            kernel, out_shape=out_shape, in_specs=specs,
            out_specs=jax.tree.map(lambda _: pl.BlockSpec(memory_space=space), out_shape),
            scratch_shapes=scratch, compiler_params=params, cost_estimate=cost,
        )(*operands)

    return run


def se_scratch(rows):
    return [
        pltpu.VMEM((rows, LANES), jnp.float32),
        pltpu.VMEM((SHORT_TAPS - 1, rows, LANES), jnp.float32),
        pltpu.VMEM((PAD + rows, LANES), jnp.float32),
        pltpu.VMEM((PAD + rows, LANES), jnp.float32),
        pltpu.VMEM((rows, LANES), jnp.float32),
        pltpu.VMEM((rows, LANES), jnp.float32),
    ]


def se_own_call(x, *rest):
    own, width = x.shape
    shapes = (jax.ShapeDtypeStruct((own, width), jnp.bfloat16), jax.ShapeDtypeStruct((1, own), jnp.float32))
    return call(se_own_kernel, shapes, se_scratch(own), 25 << 20, 2 << 20)(x, *rest)


def se_halo_call(x, *rest):
    own, width = x.shape
    rows = HALO + CHUNK
    shapes = (jax.ShapeDtypeStruct((rows, width), jnp.bfloat16), jax.ShapeDtypeStruct((1, 2 * own), jnp.float32))
    return call(se_halo_kernel, shapes, se_scratch(rows), 25 << 20, 2 << 20)(x, *rest)


def mr_call(early, mid, *rest):
    own, width = mid.shape
    ext = HALO + own
    blocks = own // LANES
    slot = [
        pltpu.VMEM((LANES, own + LANES), jnp.bfloat16),
        pltpu.VMEM((own, LANES), jnp.float32),
    ]
    scratch = [
        pltpu.VMEM((own, width), jnp.bfloat16),
        pltpu.SemaphoreType.DMA((width // (2 * LANES),)),
        pltpu.VMEM((ext, LANES), jnp.float32),
        pltpu.VMEM((FEAT_TAPS - 1, ext, LANES), jnp.float32),
        pltpu.VMEM((PAD + ext, LANES), jnp.float32),
        *slot,
        *slot,
    ]
    return call(mr_kernel, jax.ShapeDtypeStruct((own, width), jnp.bfloat16), scratch, 1 << 30, 4 << 20, space=pl.ANY)(early, mid, *rest)


def shards(hidden, doc_lengths, gain_se, gain_mr, feat_se, feat_mr, filter_se, filter_mr):
    f32 = jnp.float32
    shape = jax.ShapeDtypeStruct
    own, width = hidden.shape[1:]
    groups = filter_se.shape[0]
    x = hidden[0]
    first = (lax.axis_index("ctx") * own).astype(jnp.int32).reshape(1)
    halo = shifted(x[own - HALO :], "ctx", 1)
    part = call(sums_kernel, shape((1, own), f32), [], 1 << 20, 1 << 20)(x)
    total = part + turned(part, "tp", 3) + turned(part, "tp", 2) + turned(part, "tp", 1)
    before = shifted(total, "ctx", 1)
    ext = HALO + own
    off, fexp = call(
        place_kernel,
        (shape((ext, LANES), f32), shape((8, width), f32)),
        [], 1 << 24, 1 << 20, smem=1,
    )(first, doc_lengths, filter_se)
    base, keep = call(
        turn_kernel,
        (shape((groups, GROUP, LANES), jnp.bfloat16), shape((2 * LANES, own), jnp.bfloat16)),
        [pltpu.VMEM((groups, LANES), f32)], 1 << 24, 1 << 20,
    )(total, filter_mr, off)
    gain = gain_se.reshape(1, width)
    mid, part_two = se_own_call(x, total, off, gain, feat_se, fexp)
    early, part_two = se_halo_call(x, halo, total, before, part_two, off, gain, feat_se, fexp)
    sums_two = [part_two] + [turned(part_two, "tp", by) for by in (3, 2, 1)]
    return mr_call(early, mid, *sums_two, off, gain_mr.reshape(1, width), feat_mr, base, keep)[None]


def solution(mesh):
    in_specs = (
        P(None, "ctx", "tp"),
        P(),
        P("tp"),
        P("tp"),
        P(None, None, "tp"),
        P(None, None, "tp"),
        P("tp", None),
        P("tp", None),
    )
    out_specs = P(None, "ctx", "tp")
    return jax.shard_map(shards, mesh=mesh, in_specs=in_specs, out_specs=out_specs, check_vma=False)
```
